128 devices in a mesh: region: 8 (over z, core), member: 16 (over x, y).
Axes of the slice: x: 4, y: 4, z: 4, core: 2. Of those that a mesh axis runs over, the one named last changes fastest.
Arguments:
- velocity: float32 [8, 3, 131072], P(None, None, ('region', 'member')), may hold values from -6 to 6
- normals: float32 [3, 131072], P(None, ('region', 'member')), may hold values from -6 to 6
- areas: float32 [131072], P(('region', 'member')), may hold values from 0.3 to 3
- panel_nodes: int32 [131072, 4], P(('region', 'member')), may hold values from 0 to 16383, as said below
- near_blocks: bfloat16 [2048, 64, 1024], P(('region', 'member')), may hold values from -0.1875 to 0.1875
- near_cols: int32 [2048, 16], P(('region', 'member')), may hold values from 0 to 255, as said below
- near_count: int32 [2048], P(('region', 'member')), may hold values from 1 to 16
- basis_v: bfloat16 [2048, 64, 16], P(('region', 'member')), may hold values from -0.75 to 0.75
- basis_u: float32 [2048, 64, 16], P(('region', 'member')), may hold values from -1.5 to 1.5
- coupling: float32 [2048, 32, 16, 16], P(('region', 'member')), may hold values from -0.25 to 0.25
- far_cols: int32 [2048, 32], P(('region', 'member')), may hold values from 0 to 2047
Outputs:
- node_forces: float32 [8, 3, 131072], P(None, None, ('region', 'member'))
The draws below stay inside these ranges and needn't reach their ends.
Inputs may be any that keep to these rules, and one draw needn't show every extreme that they name: `panel_nodes`: A panel's nodes lie mostly in the node range of the member that holds the panel, some in the ranges of the members beside it (the first and last members count as beside each other), a few anywhere in the region. `near_cols`: A cluster's near slots name mostly clusters of its own member, some of the members beside it (the first and last members count as beside each other), a few anywhere in the region.
All inputs are finite; a program needn't handle non-finite values.
Results may differ from the reference program's by a relative error of at most 0.0029.
Values may be sent and summed in bfloat16 or wider, within the bound.
A program may use at most 64 MiB of HBM per device.

```python
import math
import jax
import jax.numpy as jnp
from jax import lax

BLOCK = 64
RANK = 16
LOADS = 8
NEAR = 16
FAR = 32
C_DEV = 16
NODE_DEV = 1024
C_ALL = 2048
PANELS = 131072
NODES = 131072
N_REGION = 8
N_MEMBER = 16


def local_pick(key, rows, cols, per_member, span):
    key_kind, key_side, key_other, key_offset = jax.random.split(key, 4)
    member = jnp.arange(rows, dtype=jnp.int32)[:, None] // per_member % N_MEMBER
    kind = jax.random.randint(key_kind, (rows, cols), 0, 10)
    side = jnp.where(jax.random.randint(key_side, (rows, cols), 0, 2) == 0, -1, 1)
    other = jax.random.randint(key_other, (rows, cols), 0, N_MEMBER)
    owner = jnp.where(kind < 8, member, jnp.where(kind == 8, (member + side + N_MEMBER) % N_MEMBER, other))
    offset = jax.random.randint(key_offset, (rows, cols), 0, span)
    picked = (owner * span + offset).astype(jnp.int32)
    picked = picked.at[0, 0].set(0)
    picked = picked.at[rows - 1, cols - 1].set(span * N_MEMBER - 1)
    return picked


def draw_panel_nodes(key, part):
    key = jax.random.fold_in(key, 11)
    return local_pick(key, PANELS, 4, C_DEV * BLOCK, NODE_DEV)


def draw_near_cols(key, part):
    key = jax.random.fold_in(key, 23)
    return local_pick(key, C_ALL, NEAR, C_DEV, C_DEV)


def with_ends(drawn, key, low, largest):
    longest = drawn.shape.index(max(drawn.shape))
    spots = []
    for shift in (0, 1):
        where = [jax.random.randint(jax.random.fold_in(key, axis), (), 0, length) for axis, length in enumerate(drawn.shape)]
        where[longest] = (where[longest] + shift) % drawn.shape[longest]
        spots.append(tuple(where))
    return drawn.at[spots[0]].set(low).at[spots[1]].set(largest)


def level_of(own_key, extent, pieces, least, top_value):
    level = 1.0
    for dim, blocks in pieces:
        heights = jax.random.uniform(jax.random.fold_in(jax.random.fold_in(own_key, 6), dim), (blocks,), jnp.float32, least / len(pieces), top_value / len(pieces))
        level = level * jnp.repeat(jnp.exp(heights), extent[dim] // blocks).reshape((-1,) + (1,) * (len(extent) - 1 - dim))
    return level


def bell_draw(stream_key, extent, deviation, reach, cuts=(), kind=jnp.bfloat16):
    values = jax.random.normal(stream_key, extent, jnp.float32) * deviation
    if len(cuts) > 0:
        values = level_of(stream_key, extent, cuts, -0.22, 0.18) * values
    return jnp.clip(values, min=-reach, max=reach).astype(kind)


def setup_inputs(seed: int = 0) -> dict:
    seeds = jax.random.split(jax.random.key(seed), 12)
    return {
        "velocity": bell_draw(seeds[0], (LOADS, 3, NODES), 1.0, 6.0, ((2, 128),), jnp.float32),
        "normals": bell_draw(seeds[1], (3, PANELS), 1.0, 6.0, ((1, 128),), jnp.float32),
        "areas": jnp.clip(jnp.exp(math.log(3.0) - 2.3025851 * jax.random.uniform(seeds[2], (PANELS,), jnp.float32) ** level_of(seeds[2], (PANELS,), ((0, 128),), -0.2, 0.2)), 0.3, 3.0),
        "panel_nodes": draw_panel_nodes(jax.random.fold_in(seeds[11], 71), 0),
        "near_blocks": bell_draw(seeds[4], (C_ALL, BLOCK, NEAR * BLOCK), (BLOCK * NEAR) ** -0.5, 0.1875, ((0, 128),)),
        "near_cols": draw_near_cols(jax.random.fold_in(seeds[11], 71), 0),
        "near_count": with_ends(jax.random.randint(seeds[6], (C_ALL,), 1, NEAR + 1), jax.random.fold_in(seeds[6], 1), 1, NEAR).astype(jnp.int32),
        "basis_v": bell_draw(seeds[7], (C_ALL, BLOCK, RANK), BLOCK ** -0.5, 0.75, ((0, 128),)),
        "basis_u": bell_draw(seeds[8], (C_ALL, BLOCK, RANK), RANK ** -0.5, 1.5, ((0, 128),), jnp.float32),
        "coupling": bell_draw(seeds[9], (C_ALL, FAR, RANK, RANK), (RANK * FAR) ** -0.5, 0.25, ((0, 128),), jnp.float32),
        "far_cols": with_ends(jax.random.randint(seeds[10], (C_ALL, FAR), 0, C_ALL), jax.random.fold_in(seeds[10], 1), 0, C_ALL - 1).astype(jnp.int32),
    }


def reference(velocity, normals, areas, panel_nodes, near_blocks, near_cols, near_count, basis_v, basis_u, coupling, far_cols):
    hi = lax.Precision.HIGHEST
    c_region = C_DEV * N_MEMBER
    c_total = c_region * N_REGION
    node_region = C_DEV * BLOCK * N_MEMBER
    panel_count = c_total * BLOCK
    region_of_panel = (jnp.arange(panel_count) // (c_region * BLOCK)).astype(jnp.int32)
    node_index = panel_nodes + (region_of_panel * node_region)[:, None]
    moved = jnp.zeros((LOADS, 3, panel_count), jnp.float32)
    for corner in range(4):
        moved = moved + velocity[:, :, node_index[:, corner]]
    normal_vel = 0.25 * jnp.sum(moved * normals[None], axis=1)
    density = normal_vel.astype(jnp.bfloat16)
    blocked = density.reshape(LOADS, c_total, BLOCK)
    region_of_cluster = (jnp.arange(c_total) // c_region).astype(jnp.int32)
    source_near = near_cols + (region_of_cluster * c_region)[:, None]
    used = jnp.arange(NEAR)[None, :] < near_count[:, None]
    groups = N_REGION * N_MEMBER

    def near_group(args):
        blocks, sources, usage = args
        picked = blocked[:, sources, :].astype(jnp.float32)
        picked = jnp.where(usage[None, :, :, None], picked, 0.0)
        picked = picked.reshape(LOADS, C_DEV, NEAR * BLOCK)
        return jnp.einsum("tak,ltk->lta", blocks.astype(jnp.float32), picked, precision=hi)

    near_pot = lax.map(near_group, (near_blocks.reshape(groups, C_DEV, BLOCK, NEAR * BLOCK),
                                    source_near.reshape(groups, C_DEV, NEAR), used.reshape(groups, C_DEV, NEAR)))
    near_pot = jnp.moveaxis(near_pot, 0, 1).reshape(LOADS, c_total, BLOCK)
    coeff = jnp.einsum("tbr,ltb->rlt", basis_v.astype(jnp.float32), blocked.astype(jnp.float32), precision=hi)
    gathered = coeff[:, :, far_cols]
    far_coef = jnp.einsum("tarq,qlta->rlt", coupling, gathered, precision=hi)
    far_pot = jnp.einsum("tbr,rlt->ltb", basis_u, far_coef, precision=hi)
    potential = (near_pot + far_pot).reshape(LOADS, panel_count)
    load = -0.25 * potential[:, None, :] * (areas[None, :] * normals)[None]
    node_forces = jnp.zeros((LOADS, 3, velocity.shape[2]), jnp.float32)
    for corner in range(4):
        node_forces = node_forces.at[:, :, node_index[:, corner]].add(load)
    return node_forces
```

```python
import functools

import jax
import jax.numpy as jnp
from jax import lax
from jax.experimental import pallas as pl
from jax.experimental.pallas import tpu as pltpu
from jax.sharding import PartitionSpec as P

MESH = pl.DeviceIdType.MESH
F32 = jnp.float32
BF16 = jnp.bfloat16
NT = (((1,), (1,)), ((), ()))


def split(x):
    high = x.astype(BF16)
    return high, (x - high.astype(F32)).astype(BF16)


def dot(a, b):
    return jnp.dot(a, b, preferred_element_type=F32)


def dot_nt(a, b):
    return lax.dot_general(a, b, NT, preferred_element_type=F32)


def kernel(
    regions,
    members,
    near_cols,
    near_count,
    far_cols,
    velocity,
    normals,
    areas,
    nodes,
    basis_v,
    basis_u,
    near_hbm,
    coupling_hbm,
    out,
    near,
    coupling,
    hot,
    motion,
    motion_cat,
    motion_low,
    moved,
    dens,
    table,
    coeffs,
    coeff_rows,
    picked_rows,
    coup_cat,
    folded,
    basis_v_wide,
    basis_u_high,
    basis_u_low,
    near_pot,
    spread_high,
    spread_low,
    force_out,
    force_in,
    load_sems,
    motion_sems,
    dens_sems,
    coeff_sems,
    column_sems,
    force_sems,
):
    region = lax.axis_index("region")
    me = lax.axis_index("member")
    clusters, block = near.shape[0], near.shape[1]
    panels = nodes.shape[1]
    loads = velocity.shape[1]

    def member_at(step):
        return lax.rem(me + step, members)

    near_load = pltpu.make_async_copy(near_hbm, near, load_sems.at[0])
    coup_load = pltpu.make_async_copy(coupling_hbm, coupling, load_sems.at[1])
    near_load.start()
    coup_load.start()

    barrier = pltpu.get_barrier_semaphore()
    for step in range(1, members):
        pl.semaphore_signal(barrier, inc=1, device_id=(region, member_at(step)), device_id_type=MESH)
    for step in range(1, regions):
        pl.semaphore_signal(
            barrier, inc=1, device_id=(lax.rem(region + step, regions), me), device_id_type=MESH
        )

    def push(source, target, sems, step):
        return pltpu.make_async_remote_copy(
            src_ref=source,
            dst_ref=target,
            send_sem=sems.at[0, step],
            recv_sem=sems.at[1, step],
            device_id=(region, member_at(step)),
            device_id_type=MESH,
        )

    own = jnp.concatenate(
        [velocity[c, :, lo * 128 : (lo + 1) * 128] for lo in range(8) for c in range(3)], axis=0
    )
    own_high, own_low = split(own)
    motion[me] = own_high
    motion_low[...] = own_low
    pl.semaphore_wait(barrier, members - 1 + regions - 1)
    motion_push = [push(motion.at[me], motion.at[me], motion_sems, s) for s in range(1, members)]
    for copy in motion_push:
        copy.start()

    node = [nodes[k : k + 1, :] for k in range(4)]
    lane_of = jnp.concatenate(
        [((n >> 10) << 7) | (n & 127) for n in node], axis=1
    )

    @pl.loop(0, hot.shape[0] // 16)
    def _(i):
        base = pl.multiple_of(i * 16, 16)
        rows = lax.broadcasted_iota(jnp.int32, (16, 4 * panels), 0) + base
        hot[pl.ds(base, 16), :] = jnp.where(rows == lane_of, 1.0, 0.0).astype(BF16)

    for g in range(clusters // 2):
        pair = jnp.concatenate([basis_v[2 * g], basis_v[2 * g + 1]], axis=1)
        basis_v_wide[:, g * 128 : (g + 1) * 128] = jnp.concatenate([pair] * loads, axis=0)
    basis_u_high[...] = jnp.zeros_like(basis_u_high)
    basis_u_low[...] = jnp.zeros_like(basis_u_low)
    empty = jnp.zeros((16, block), F32)
    for t in range(clusters):
        parts = [basis_u[t], empty] if t % 2 == 0 else [empty, basis_u[t]]
        high, low = split(jnp.concatenate(parts, axis=1))
        where = (slice(t * 16, t * 16 + 16), slice(t // 2 * 128, t // 2 * 128 + 128))
        basis_u_high[where] = high
        basis_u_low[where] = low
    coup_load.wait()

    @pl.loop(0, clusters)
    def _(t):
        high, low = split(coupling[t].reshape(256, 32))
        coup_cat[t] = jnp.concatenate([high, low], axis=1)

    table[table.shape[0] - 1] = jnp.zeros((8, 128), F32)

    for copy in motion_push:
        copy.wait_recv()
    for m in range(members):
        motion_cat[:, m * 128 : (m + 1) * 128] = motion[m]
    own_rows = pl.ds(pl.multiple_of(me * 128, 128), 128)

    @pl.loop(0, panels // 256)
    def _(i):
        base = pl.multiple_of(i * 256, 256)
        total = [jnp.zeros((8, 256), F32) for _ in range(3)]
        for k in range(4):
            columns = pl.ds(k * panels + base, 256)
            rows = dot(motion_cat[...], hot[:, columns]) + dot(motion_low[...], hot[own_rows, columns])
            lo = (nodes[k : k + 1, pl.ds(base, 256)] >> 7) & 7
            for q in range(8):
                hit = jnp.broadcast_to(lo == q, (8, 256))
                for c in range(3):
                    at = (q * 3 + c) * 8
                    total[c] = total[c] + jnp.where(hit, rows[at : at + 8], 0.0)
        for c in range(3):
            moved[c, :, pl.ds(base, 256)] = total[c]

    normal_vel = 0.25 * (
        moved[0] * normals[0:1, :] + moved[1] * normals[1:2, :] + moved[2] * normals[2:3, :]
    )
    density = normal_vel.astype(BF16).astype(F32)
    half = panels // 2
    dens[me] = jnp.concatenate([density[:, :half], density[:, half:]], axis=0).astype(BF16)
    dens_push = [push(dens.at[me], dens.at[me], dens_sems, s) for s in range(1, members)]
    lane_cluster = lax.broadcasted_iota(jnp.int32, (8, panels), 1) // block
    diagonal = jnp.concatenate(
        [jnp.where(lane_cluster == t, density, 0.0) for t in range(clusters)], axis=0
    ).astype(BF16)
    wide = dot_nt(diagonal, basis_v_wide[...])
    row_load = lax.broadcasted_iota(jnp.int32, (128, 128), 0) & 7
    lane_load = lax.broadcasted_iota(jnp.int32, (128, 128), 1) >> 4
    wide = jnp.where(row_load == lane_load, wide, 0.0)
    coeffs[me, region] = jnp.sum(wide.reshape(clusters, 8, 128), axis=1).astype(BF16)
    column_push = [
        pltpu.make_async_remote_copy(
            src_ref=coeffs.at[me, region],
            dst_ref=coeffs.at[me, region],
            send_sem=column_sems.at[0, s],
            recv_sem=column_sems.at[1, s],
            device_id=(lax.rem(region + s, regions), me),
            device_id_type=MESH,
        )
        for s in range(1, regions)
    ]
    for copy in column_push:
        copy.start()
    for copy in dens_push:
        copy.start()
    for copy in column_push:
        copy.wait_recv()
    coeff_push = [push(coeffs.at[me], coeffs.at[me], coeff_sems, s) for s in range(1, members)]
    for copy in coeff_push:
        copy.start()

    near_load.wait()
    for copy in dens_push:
        copy.wait_recv()
    left = lax.broadcasted_iota(jnp.int32, (8, 128), 1) < block

    @pl.loop(0, members)
    def _(m):
        rows = dens[m].astype(F32)
        for h in range(2):
            for g in range(half // 128):
                both = rows[h * 8 : h * 8 + 8, g * 128 : (g + 1) * 128]
                turned = pltpu.roll(both, block, axis=1)
                at = m * clusters + h * (clusters // 2) + g * 2
                table[at] = jnp.where(left, both, turned)
                table[at + 1] = jnp.where(left, turned, both)

    slots = near_cols.shape[1]
    unused = table.shape[0] - 1

    @pl.loop(0, clusters // 2)
    def _(g):
        picked = []
        for h in range(2):
            t = 2 * g + h
            count = near_count[t]
            parts = []
            for j in range(0, slots, 2):
                first = jnp.where(j < count, near_cols[t, j], unused)
                second = jnp.where(j + 1 < count, near_cols[t, j + 1], unused)
                parts.append(jnp.where(left, table[first], table[second]))
            picked.append(jnp.concatenate(parts, axis=1))
        both = jnp.concatenate(picked, axis=0).astype(BF16)
        blocks = near[pl.ds(2 * g, 2)].reshape(2 * block, slots * block)
        result = dot_nt(both, blocks)
        near_pot[:, pl.ds(pl.multiple_of(g * 128, 128), 128)] = jnp.where(left, result[:8], result[8:])

    for copy in coeff_push:
        copy.wait_recv()

    @pl.loop(0, members)
    def _(m):
        for r in range(regions):
            at = pl.multiple_of((r * members + m) * clusters, clusters)
            coeff_rows[pl.ds(at, clusters), :] = coeffs[m, r].astype(F32)

    own_q = lax.broadcasted_iota(jnp.int32, (256, 128), 0) & 15
    lane_q = lax.broadcasted_iota(jnp.int32, (256, 128), 1) & 15
    same_q = own_q == lane_q

    @pl.loop(0, clusters)
    def _(t):
        for a in range(32):
            picked_rows[pl.ds(a, 1), :] = coeff_rows[pl.ds(far_cols[t, a], 1), :]
        rows = picked_rows[...].astype(BF16)
        product = dot(coup_cat[t], jnp.concatenate([rows, rows], axis=0))
        product = jnp.where(same_q, product, 0.0)
        folded[pl.ds(pl.multiple_of(t * 16, 16), 16), :] = jnp.sum(
            product.reshape(16, 16, 128), axis=1
        )

    fold = jnp.where(
        lax.broadcasted_iota(jnp.int32, (8, 128), 0)
        == lax.broadcasted_iota(jnp.int32, (8, 128), 1) >> 4,
        1.0,
        0.0,
    )
    fold = jnp.concatenate([fold, fold], axis=0).astype(BF16)
    folded_high, folded_low = split(folded[...])
    far_coef = (dot_nt(fold, folded_high) + dot_nt(fold, folded_low))[:8]
    far_high, far_low = split(far_coef)
    far_both = jnp.concatenate([far_high.astype(F32), far_low.astype(F32)], axis=0).astype(BF16)
    with_high = dot(far_both, basis_u_high[...])
    with_low = dot(far_both, basis_u_low[...])
    potential = near_pot[...] + (with_high[:8] + with_high[8:] + with_low[:8])

    scaled = -0.25 * areas[...]
    for c in range(3):
        moved[c] = potential * (scaled * normals[c : c + 1, :])

    @pl.loop(0, panels // 256)
    def _(i):
        base = pl.multiple_of(i * 256, 256)
        load = [moved[c, :, pl.ds(base, 256)] for c in range(3)]
        for k in range(4):
            lo = (nodes[k : k + 1, pl.ds(base, 256)] >> 7) & 7
            rows = []
            for q in range(8):
                hit = jnp.broadcast_to(lo == q, (8, 256))
                rows += [jnp.where(hit, load[c], 0.0) for c in range(3)]
            high, low = split(jnp.concatenate(rows, axis=0))
            columns = pl.ds(k * panels + base, 256)
            spread_high[:, columns] = high
            spread_low[:, columns] = low

    pairs = members // 2
    pair = me // 2

    @pl.loop(1, pairs)
    def _(i):
        other = lax.rem(pair + i, pairs)
        rows = hot[pl.ds(pl.multiple_of(other * 256, 256), 256), :]
        sums = dot_nt(spread_high[...], rows).astype(BF16)
        for h in range(2):
            target = 2 * other + h
            step = lax.rem(target - me + members, members)
            force_out[target] = sums[:, h * 128 : (h + 1) * 128]
            push_force(force_out, force_in, force_sems, region, me, target, step).start()

    partner = me + 1 - 2 * lax.rem(me, 2)
    partner_rows = pl.ds(pl.multiple_of(partner * 128, 128), 128)
    force_out[partner] = dot_nt(spread_high[...], hot[partner_rows, :]).astype(BF16)
    step = lax.rem(partner - me + members, members)
    push_force(force_out, force_in, force_sems, region, me, partner, step).start()
    mine = hot[own_rows, :]
    total = dot_nt(spread_high[...], mine) + dot_nt(spread_low[...], mine)
    for step in range(1, members):
        source = lax.rem(me - step + members, members)
        push_force(force_out, force_in, force_sems, region, me, member_at(step), step).wait_recv()
        total = total + force_in[source].astype(F32)
    for lo in range(8):
        for c in range(3):
            at = (lo * 3 + c) * 8
            out[c, :, lo * 128 : (lo + 1) * 128] = total[at : at + 8]

    for copy in motion_push + dens_push + column_push + coeff_push:
        copy.wait_send()
    for step in range(1, members):
        push_force(force_out, force_in, force_sems, region, me, member_at(step), step).wait_send()


def push_force(force_out, force_in, sems, region, me, target, step):
    return pltpu.make_async_remote_copy(
        src_ref=force_out.at[target],
        dst_ref=force_in.at[me],
        send_sem=sems.at[0, step],
        recv_sem=sems.at[1, step],
        device_id=(region, target),
        device_id_type=MESH,
    )


def body(
    regions,
    members,
    velocity,
    normals,
    areas,
    panel_nodes,
    near_blocks,
    near_cols,
    near_count,
    basis_v,
    basis_u,
    coupling,
    far_cols,
):
    nodes = velocity.shape[2]
    panels = normals.shape[1]
    clusters, block = near_blocks.shape[0], near_blocks.shape[1]
    rows = 24 * nodes // 128
    lanes = members * 128
    smem = pl.BlockSpec(memory_space=pltpu.SMEM)
    vmem = pl.BlockSpec(memory_space=pltpu.VMEM)
    hbm = pl.BlockSpec(memory_space=pl.ANY)
    dma = pltpu.SemaphoreType.DMA
    result = pl.pallas_call(
        functools.partial(kernel, regions, members),
        out_shape=jax.ShapeDtypeStruct((3, 8, nodes), F32),
        in_specs=[smem] * 3 + [vmem] * 6 + [hbm] * 2,
        out_specs=vmem,
        scratch_shapes=[
            pltpu.VMEM(near_blocks.shape, BF16),
            pltpu.VMEM((clusters, 16, 16, 32), F32),
            pltpu.VMEM((lanes, 4 * panels), BF16),
            pltpu.VMEM((members, rows, 128), BF16),
            pltpu.VMEM((rows, lanes), BF16),
            pltpu.VMEM((rows, 128), BF16),
            pltpu.VMEM((3, 8, panels), F32),
            pltpu.VMEM((members, 16, panels // 2), BF16),
            pltpu.VMEM((members * clusters + 1, 8, 128), F32),
            pltpu.VMEM((members, regions, clusters, 128), BF16),
            pltpu.VMEM((members * regions * clusters, 128), F32),
            pltpu.VMEM((32, 128), F32),
            pltpu.VMEM((clusters, 256, 64), BF16),
            pltpu.VMEM((clusters * 16, 128), F32),
            pltpu.VMEM((128, panels), BF16),
            pltpu.VMEM((clusters * 16, panels), BF16),
            pltpu.VMEM((clusters * 16, panels), BF16),
            pltpu.VMEM((8, panels), F32),
            pltpu.VMEM((rows, 4 * panels), BF16),
            pltpu.VMEM((rows, 4 * panels), BF16),
            pltpu.VMEM((members, rows, 128), BF16),
            pltpu.VMEM((members, rows, 128), BF16),
            dma((2,)),
            dma((2, members)),
            dma((2, members)),
            dma((2, members)),
            dma((2, regions)),
            dma((2, members)),
        ],
        compiler_params=pltpu.CompilerParams(
            collective_id=0, has_side_effects=True, vmem_limit_bytes=56 * 1024 * 1024
        ),
        name="hull",
    )(
        near_cols,
        near_count,
        far_cols,
        jnp.transpose(velocity, (1, 0, 2)),
        normals,
        areas.reshape(1, panels),
        panel_nodes.T,
        jnp.transpose(basis_v, (0, 2, 1)),
        jnp.transpose(basis_u, (0, 2, 1)),
        near_blocks,
        jnp.transpose(coupling, (0, 2, 3, 1)),
    )
    return jnp.transpose(result, (1, 0, 2))


def solution(mesh):
    both = ("region", "member")
    placed = (
        P(None, None, both),
        P(None, both),
        P(both),
        P(both, None),
        P(both, None, None),
        P(both, None),
        P(both),
        P(both, None, None),
        P(both, None, None),
        P(both, None, None, None),
        P(both, None),
    )
    return jax.shard_map(
        functools.partial(body, mesh.shape["region"], mesh.shape["member"]),
        mesh=mesh,
        in_specs=placed,
        out_specs=P(None, None, both),
        check_vma=False,
    )
```

```python
import functools

import jax
import jax.numpy as jnp
from jax import lax
from jax.experimental import pallas as pl
from jax.experimental.pallas import tpu as pltpu
from jax.sharding import PartitionSpec as P

MESH = pl.DeviceIdType.MESH
F32 = jnp.float32
BF16 = jnp.bfloat16
NT = (((1,), (1,)), ((), ()))


def split(x):
    high = x.astype(BF16)
    return high, (x - high.astype(F32)).astype(BF16)


def dot(a, b):
    return jnp.dot(a, b, preferred_element_type=F32)


def dot_nt(a, b):
    return lax.dot_general(a, b, NT, preferred_element_type=F32)


def kernel(
    regions,
    members,
    near_cols,
    near_count,
    far_cols,
    velocity,
    normals,
    areas,
    nodes,
    basis_v,
    basis_u,
    near_hbm,
    coupling_hbm,
    out,
    near,
    coupling,
    hot,
    hot_turned,
    column_of,
    motion,
    motion_cat,
    motion_low,
    moved,
    dens,
    table,
    coeffs,
    coeff_rows,
    picked_rows,
    coup_cat,
    folded,
    basis_v_wide,
    basis_u_high,
    basis_u_low,
    near_pot,
    spread_high,
    spread_low,
    force_near,
    force_out,
    force_in,
    load_sems,
    motion_sems,
    dens_sems,
    coeff_sems,
    force_sems,
    ready,
):
    region = lax.axis_index("region")
    me = lax.axis_index("member")
    clusters, block = near.shape[0], near.shape[1]
    panels = nodes.shape[1]
    loads = velocity.shape[1]

    def member_at(step):
        return lax.rem(me + step, members)

    near_load = pltpu.make_async_copy(near_hbm, near, load_sems.at[0])
    coup_load = pltpu.make_async_copy(coupling_hbm, coupling, load_sems.at[1])
    near_load.start()
    coup_load.start()

    barrier = pltpu.get_barrier_semaphore()
    for step in range(1, members):
        pl.semaphore_signal(barrier, inc=1, device_id=(region, member_at(step)), device_id_type=MESH)
    for step in range(1, regions):
        pl.semaphore_signal(
            barrier, inc=1, device_id=(lax.rem(region + step, regions), me), device_id_type=MESH
        )

    def push(source, target, sems, step):
        return push_to(source, target, sems, region, member_at(step))

    def push_all(rows, sems):
        @pl.loop(1, members)
        def _(step):
            push(rows.at[me], rows.at[me], sems, step).start()

    def pushed(rows, sems):
        part = rows.at[pl.ds(0, members - 1)]
        return push(part, part, sems, 1)

    own = jnp.concatenate(
        [velocity[c, :, lo * 128 : (lo + 1) * 128] for lo in range(8) for c in range(3)], axis=0
    )
    own_high, own_low = split(own)
    motion[me] = own_high
    motion_low[...] = own_low
    pl.semaphore_wait(barrier, members - 1 + regions - 1)
    push_all(motion, motion_sems)
    for step in range(1, regions):
        pl.semaphore_signal(
            ready, inc=1, device_id=(lax.rem(region + step, regions), me), device_id_type=MESH
        )

    node = nodes[...]
    lanes_low, owner = (node & 127).astype(F32), (node >> 10).astype(F32)
    column_of[...] = jnp.transpose(jnp.concatenate([lanes_low, owner], axis=0))
    one, zero = jnp.ones((), BF16), jnp.zeros((), BF16)

    @pl.loop(0, 8)
    def _(i):
        base = pl.multiple_of(i * 16, 16)
        rows = (lax.broadcasted_iota(jnp.int32, (16, panels), 0) + base).astype(F32).astype(BF16)
        for k in range(4):
            low = jnp.broadcast_to(lanes_low[k : k + 1], (16, panels)).astype(BF16)
            holder = jnp.broadcast_to(owner[k : k + 1], (16, panels)).astype(BF16)
            found = jnp.where(low == rows, one, zero)
            for m in range(members):
                hot[pl.ds(m * 128 + base, 16), k * panels : (k + 1) * panels] = jnp.where(
                    holder == float(m), found, zero
                )

    @pl.loop(0, panels // 16)
    def _(i):
        base = pl.multiple_of(i * 16, 16)
        lanes = lax.broadcasted_iota(jnp.int32, (16, 128), 1).astype(F32).astype(BF16)
        for k in range(4):
            low = jnp.broadcast_to(column_of[pl.ds(base, 16), k : k + 1], (16, 128)).astype(BF16)
            holder = jnp.broadcast_to(column_of[pl.ds(base, 16), k + 4 : k + 5], (16, 128)).astype(BF16)
            found = jnp.where(low == lanes, one, zero)
            for m in range(members):
                hot_turned[pl.ds(k * panels + base, 16), m * 128 : (m + 1) * 128] = jnp.where(
                    holder == float(m), found, zero
                )

    for g in range(clusters // 2):
        pair = jnp.concatenate([basis_v[2 * g], basis_v[2 * g + 1]], axis=1)
        basis_v_wide[:, g * 128 : (g + 1) * 128] = jnp.concatenate([pair] * loads, axis=0)
    basis_u_high[...] = jnp.zeros_like(basis_u_high)
    basis_u_low[...] = jnp.zeros_like(basis_u_low)
    empty = jnp.zeros((16, block), F32)
    for t in range(clusters):
        parts = [basis_u[t], empty] if t % 2 == 0 else [empty, basis_u[t]]
        high, low = split(jnp.concatenate(parts, axis=1))
        where = (slice(t * 16, t * 16 + 16), slice(t // 2 * 128, t // 2 * 128 + 128))
        basis_u_high[where] = high
        basis_u_low[where] = low
    coup_load.wait()

    @pl.loop(0, clusters)
    def _(t):
        high, low = split(coupling[t].reshape(256, 32))
        coup_cat[t] = jnp.concatenate([high, low], axis=1)

    table[table.shape[0] - 1] = jnp.zeros((8, 128), F32)

    pushed(motion, motion_sems).wait_recv()
    for m in range(members):
        motion_cat[:, m * 128 : (m + 1) * 128] = motion[m]
    own_rows = pl.ds(pl.multiple_of(me * 128, 128), 128)

    for c in range(3):
        moved[c] = jnp.zeros((8, panels), F32)

    @pl.loop(0, 4)
    def _(k):
        columns = pl.ds(pl.multiple_of(k * panels, panels), panels)
        rows = dot(motion_cat[...], hot[:, columns]) + dot(motion_low[...], hot[own_rows, columns])
        lo = (nodes[pl.ds(k, 1), :] >> 7) & 7
        for c in range(3):
            total = moved[c]
            for q in range(8):
                at = (q * 3 + c) * 8
                total = total + jnp.where(jnp.broadcast_to(lo == q, (8, panels)), rows[at : at + 8], 0.0)
            moved[c] = total

    normal_vel = 0.25 * (
        moved[0] * normals[0:1, :] + moved[1] * normals[1:2, :] + moved[2] * normals[2:3, :]
    )
    density = normal_vel.astype(BF16).astype(F32)
    half = panels // 2
    dens[me] = jnp.concatenate([density[:, :half], density[:, half:]], axis=0).astype(BF16)
    push_all(dens, dens_sems)

    lane_cluster = lax.broadcasted_iota(jnp.int32, (8, panels), 1) // block
    diagonal = jnp.concatenate(
        [jnp.where(lane_cluster == t, density, 0.0) for t in range(clusters)], axis=0
    ).astype(BF16)
    wide = dot_nt(diagonal, basis_v_wide[...])
    row_load = lax.broadcasted_iota(jnp.int32, (128, 128), 0) & 7
    lane_load = lax.broadcasted_iota(jnp.int32, (128, 128), 1) >> 4
    wide = jnp.where(row_load == lane_load, wide, 0.0)
    device = region * members + me
    coeffs[device] = jnp.sum(wide.reshape(clusters, 8, 128), axis=1).astype(BF16)
    pl.semaphore_wait(ready, regions - 1)

    @pl.loop(1, regions * members)
    def _(step):
        there = lax.rem(region + step // members, regions)
        push_to(coeffs.at[device], coeffs.at[device], coeff_sems, there, member_at(lax.rem(step, members))).start()

    near_load.wait()
    pushed(dens, dens_sems).wait_recv()
    left = lax.broadcasted_iota(jnp.int32, (8, 128), 1) < block

    @pl.loop(0, members)
    def _(m):
        rows = dens[m].astype(F32)
        for h in range(2):
            for g in range(half // 128):
                both = rows[h * 8 : h * 8 + 8, g * 128 : (g + 1) * 128]
                turned = pltpu.roll(both, block, axis=1)
                at = m * clusters + h * (clusters // 2) + g * 2
                table[at] = jnp.where(left, both, turned)
                table[at + 1] = jnp.where(left, turned, both)

    slots = near_cols.shape[1]
    unused = table.shape[0] - 1

    @pl.loop(0, clusters // 2)
    def _(g):
        picked = []
        for h in range(2):
            t = 2 * g + h
            count = near_count[t]
            parts = []
            for j in range(0, slots, 2):
                first = jnp.where(j < count, near_cols[t, j], unused)
                second = jnp.where(j + 1 < count, near_cols[t, j + 1], unused)
                parts.append(jnp.where(left, table[first], table[second]))
            picked.append(jnp.concatenate(parts, axis=1))
        both = jnp.concatenate(picked, axis=0).astype(BF16)
        blocks = near[pl.ds(2 * g, 2)].reshape(2 * block, slots * block)
        result = dot_nt(both, blocks)
        near_pot[:, pl.ds(pl.multiple_of(g * 128, 128), 128)] = jnp.where(left, result[:8], result[8:])

    coeff_part = coeffs.at[pl.ds(0, regions * members - 1)]
    coeff_pushed = push(coeff_part, coeff_part, coeff_sems, 1)
    coeff_pushed.wait_recv()

    @pl.loop(0, members)
    def _(i):
        for r in range(regions):
            d = i * regions + r
            at = pl.multiple_of(d * clusters, clusters)
            coeff_rows[pl.ds(at, clusters), :] = coeffs[d].astype(F32)

    own_q = lax.broadcasted_iota(jnp.int32, (256, 128), 0) & 15
    lane_q = lax.broadcasted_iota(jnp.int32, (256, 128), 1) & 15
    same_q = own_q == lane_q

    @pl.loop(0, clusters)
    def _(t):
        for a in range(32):
            picked_rows[pl.ds(t * 32 + a, 1), :] = coeff_rows[pl.ds(far_cols[t, a], 1), :]

    for t in range(clusters):
        rows = picked_rows[t * 32 : t * 32 + 32].astype(BF16)
        product = dot(coup_cat[t], jnp.concatenate([rows, rows], axis=0))
        product = jnp.where(same_q, product, 0.0)
        folded[t * 16 : t * 16 + 16] = jnp.sum(product.reshape(16, 16, 128), axis=1)

    fold = jnp.where(
        lax.broadcasted_iota(jnp.int32, (8, 128), 0)
        == lax.broadcasted_iota(jnp.int32, (8, 128), 1) >> 4,
        1.0,
        0.0,
    )
    fold = jnp.concatenate([fold, fold], axis=0).astype(BF16)
    folded_high, folded_low = split(folded[...])
    far_coef = (dot_nt(fold, folded_high) + dot_nt(fold, folded_low))[:8]
    far_high, far_low = split(far_coef)
    far_both = jnp.concatenate([far_high.astype(F32), far_low.astype(F32)], axis=0).astype(BF16)
    with_high = dot(far_both, basis_u_high[...])
    with_low = dot(far_both, basis_u_low[...])
    potential = near_pot[...] + (with_high[:8] + with_high[8:] + with_low[:8])

    scaled = -0.25 * areas[...]
    for c in range(3):
        moved[c] = potential * (scaled * normals[c : c + 1, :])

    @pl.loop(0, panels // 256)
    def _(i):
        base = pl.multiple_of(i * 256, 256)
        load = [moved[c, :, pl.ds(base, 256)] for c in range(3)]
        for k in range(4):
            lo = (nodes[k : k + 1, pl.ds(base, 256)] >> 7) & 7
            rows = []
            for q in range(8):
                hit = jnp.broadcast_to(lo == q, (8, 256))
                rows += [jnp.where(hit, load[c], 0.0) for c in range(3)]
            high, low = split(jnp.concatenate(rows, axis=0))
            columns = pl.ds(k * panels + base, 256)
            spread_high[:, columns] = high
            spread_low[:, columns] = low

    groups = members // 4
    group = me // 4

    @pl.loop(1, groups + 1)
    def _(i):
        other = lax.rem(group + i, groups)
        columns = pl.ds(pl.multiple_of(other * 512, 512), 512)
        sums = dot(spread_high[...], hot_turned[:, columns])
        for h in range(4):
            force_near[h] = sums[:, h * 128 : (h + 1) * 128]
        for turn in range(1, 5):
            h = lax.rem(me + turn, 4)
            target = 4 * other + h

            @pl.when(target != me)
            def _():
                force_out[target] = force_near[h].astype(BF16)
                push_to(force_out.at[target], force_in.at[me], force_sems, region, target).start()

    total = force_near[lax.rem(me, 4)] + dot(spread_low[...], hot_turned[:, own_rows])
    pushed(force_in, force_sems).wait_recv()
    for step in range(1, members):
        total = total + force_in[lax.rem(me + step, members)].astype(F32)
    for lo in range(8):
        for c in range(3):
            at = (lo * 3 + c) * 8
            out[c, :, lo * 128 : (lo + 1) * 128] = total[at : at + 8]

    pushed(motion, motion_sems).wait_send()
    pushed(dens, dens_sems).wait_send()
    coeff_pushed.wait_send()
    pushed(force_out, force_sems).wait_send()


def push_to(source, target, sems, region, member):
    return pltpu.make_async_remote_copy(
        src_ref=source,
        dst_ref=target,
        send_sem=sems.at[0],
        recv_sem=sems.at[1],
        device_id=(region, member),
        device_id_type=MESH,
    )


def body(
    regions,
    members,
    velocity,
    normals,
    areas,
    panel_nodes,
    near_blocks,
    near_cols,
    near_count,
    basis_v,
    basis_u,
    coupling,
    far_cols,
):
    nodes = velocity.shape[2]
    panels = normals.shape[1]
    clusters, block = near_blocks.shape[0], near_blocks.shape[1]
    rows = 24 * nodes // 128
    lanes = members * 128
    smem = pl.BlockSpec(memory_space=pltpu.SMEM)
    vmem = pl.BlockSpec(memory_space=pltpu.VMEM)
    hbm = pl.BlockSpec(memory_space=pl.ANY)
    dma = pltpu.SemaphoreType.DMA
    result = pl.pallas_call(
        functools.partial(kernel, regions, members),
        out_shape=jax.ShapeDtypeStruct((3, 8, nodes), F32),
        in_specs=[smem] * 3 + [vmem] * 6 + [hbm] * 2,
        out_specs=vmem,
        scratch_shapes=[
            pltpu.VMEM(near_blocks.shape, BF16),
            pltpu.VMEM((clusters, 16, 16, 32), F32),
            pltpu.VMEM((lanes, 4 * panels), BF16),
            pltpu.VMEM((4 * panels, lanes), BF16),
            pltpu.VMEM((panels, 8), F32),
            pltpu.VMEM((members, rows, 128), BF16),
            pltpu.VMEM((rows, lanes), BF16),
            pltpu.VMEM((rows, 128), BF16),
            pltpu.VMEM((3, 8, panels), F32),
            pltpu.VMEM((members, 16, panels // 2), BF16),
            pltpu.VMEM((members * clusters + 1, 8, 128), F32),
            pltpu.VMEM((members * regions, clusters, 128), BF16),
            pltpu.VMEM((members * regions * clusters, 128), F32),
            pltpu.VMEM((clusters * 32, 128), F32),
            pltpu.VMEM((clusters, 256, 64), BF16),
            pltpu.VMEM((clusters * 16, 128), F32),
            pltpu.VMEM((128, panels), BF16),
            pltpu.VMEM((clusters * 16, panels), BF16),
            pltpu.VMEM((clusters * 16, panels), BF16),
            pltpu.VMEM((8, panels), F32),
            pltpu.VMEM((rows, 4 * panels), BF16),
            pltpu.VMEM((rows, 4 * panels), BF16),
            pltpu.VMEM((4, rows, 128), F32),
            pltpu.VMEM((members, rows, 128), BF16),
            pltpu.VMEM((members, rows, 128), BF16),
            dma((2,)),
            dma((2,)),
            dma((2,)),
            dma((2,)),
            dma((2,)),
            pltpu.SemaphoreType.REGULAR,
        ],
        compiler_params=pltpu.CompilerParams(
            collective_id=0, has_side_effects=True, vmem_limit_bytes=56 * 1024 * 1024
        ),
        name="hull",
    )(
        near_cols,
        near_count,
        far_cols,
        jnp.transpose(velocity, (1, 0, 2)),
        normals,
        areas.reshape(1, panels),
        panel_nodes.T,
        jnp.transpose(basis_v, (0, 2, 1)),
        jnp.transpose(basis_u, (0, 2, 1)),
        near_blocks,
        jnp.transpose(coupling, (0, 2, 3, 1)),
    )
    return jnp.transpose(result, (1, 0, 2))


def solution(mesh):
    both = ("region", "member")
    placed = (
        P(None, None, both),
        P(None, both),
        P(both),
        P(both, None),
        P(both, None, None),
        P(both, None),
        P(both),
        P(both, None, None),
        P(both, None, None),
        P(both, None, None, None),
        P(both, None),
    )
    return jax.shard_map(
        functools.partial(body, mesh.shape["region"], mesh.shape["member"]),
        mesh=mesh,
        in_specs=placed,
        out_specs=P(None, None, both),
        check_vma=False,
    )
```

```python
import functools

import jax
import jax.numpy as jnp
from jax import lax
from jax.experimental import pallas as pl
from jax.experimental.pallas import tpu as pltpu
from jax.sharding import PartitionSpec as P

MESH = pl.DeviceIdType.MESH
F32 = jnp.float32
BF16 = jnp.bfloat16
NT = (((1,), (1,)), ((), ()))


def split(x):
    high = x.astype(BF16)
    return high, (x - high.astype(F32)).astype(BF16)


def dot(a, b):
    return jnp.dot(a, b, preferred_element_type=F32)


def dot_nt(a, b):
    return lax.dot_general(a, b, NT, preferred_element_type=F32)


def kernel(
    regions,
    members,
    near_cols,
    near_count,
    far_cols,
    velocity,
    normals,
    areas,
    nodes,
    basis_v,
    basis_u,
    near_hbm,
    coupling_hbm,
    out,
    near,
    coupling,
    hot,
    hot_turned,
    column_of,
    motion,
    motion_cat,
    motion_low,
    moved,
    dens,
    table,
    coeffs,
    coeff_rows,
    picked_rows,
    coup_cat,
    folded,
    basis_v_wide,
    basis_u_high,
    basis_u_low,
    near_pot,
    spread,
    force_out,
    upper_own,
    lower_own,
    upper_in,
    lower_in,
    last_out,
    last_in,
    load_sems,
    motion_sems,
    relay_sems,
    dens_sems,
    coeff_sems,
    side_sems,
    force_sems,
    last_sems,
    ready,
):
    region = lax.axis_index("region")
    me = lax.axis_index("member")
    x, y = me // 4, lax.rem(me, 4)
    plane, core = region // 2, lax.rem(region, 2)
    clusters, block = near.shape[0], near.shape[1]
    panels = nodes.shape[1]
    loads = velocity.shape[1]

    def member_at(step):
        return lax.rem(me + step, members)

    near_load = pltpu.make_async_copy(near_hbm, near, load_sems.at[0])
    coup_load = pltpu.make_async_copy(coupling_hbm, coupling, load_sems.at[1])
    near_load.start()
    coup_load.start()

    barrier = pltpu.get_barrier_semaphore()
    for step in range(1, members):
        pl.semaphore_signal(barrier, inc=1, device_id=(region, member_at(step)), device_id_type=MESH)
    for step in range(1, regions):
        pl.semaphore_signal(
            barrier, inc=1, device_id=(lax.rem(region + step, regions), me), device_id_type=MESH
        )

    def push(source, target, sems, step):
        return push_to(source, target, sems, region, member_at(step))

    def push_all(rows, sems):
        @pl.loop(1, members)
        def _(step):
            push(rows.at[me], rows.at[me], sems, step).start()

    def pushed(rows, sems):
        part = rows.at[pl.ds(0, members - 1)]
        return push(part, part, sems, 1)

    own = jnp.concatenate(
        [velocity[c, :, lo * 128 : (lo + 1) * 128] for lo in range(8) for c in range(3)], axis=0
    )
    own_high, own_low = split(own)
    motion[x, y] = own_high
    motion_low[...] = own_low
    pl.semaphore_wait(barrier, members - 1 + regions - 1)
    half_rows = motion.shape[2] // 2
    upper, lower = pl.ds(0, half_rows), pl.ds(half_rows, half_rows)

    def along_x(turn):
        return lax.rem(x + turn, 4) * 4 + y

    def along_y(turn):
        return x * 4 + lax.rem(y + turn, 4)

    for turn in (2, 1, 3):
        mine = motion.at[x, y, upper]
        push_to(mine, mine, motion_sems, region, along_x(turn)).start()
        mine = motion.at[x, y, lower]
        push_to(mine, mine, motion_sems, region, along_y(turn)).start()
    for step in range(1, regions):
        pl.semaphore_signal(
            ready, inc=1, device_id=(lax.rem(region + step, regions), me), device_id_type=MESH
        )

    node = nodes[...]
    lanes_low, owner = (node & 127).astype(F32), (node >> 10).astype(F32)
    ahead_x = ((node >> 12) - x) & 3
    ahead_y = (((node >> 10) & 3) - y) & 3
    stand = (((ahead_y - ahead_x + 3) & 3) * 4 + ahead_x).astype(F32)
    column_of[...] = jnp.transpose(jnp.concatenate([lanes_low, stand], axis=0))
    one, zero = jnp.ones((), BF16), jnp.zeros((), BF16)

    @pl.loop(0, 8)
    def _(i):
        base = pl.multiple_of(i * 16, 16)
        rows = (lax.broadcasted_iota(jnp.int32, (16, panels), 0) + base).astype(F32).astype(BF16)
        for k in range(4):
            low = jnp.broadcast_to(lanes_low[k : k + 1], (16, panels)).astype(BF16)
            holder = jnp.broadcast_to(owner[k : k + 1], (16, panels)).astype(BF16)
            found = jnp.where(low == rows, one, zero)
            for m in range(members):
                hot[pl.ds(m * 128 + base, 16), k * panels : (k + 1) * panels] = jnp.where(
                    holder == float(m), found, zero
                )

    firsts = motion.at[0, pl.ds(0, 3)]
    first_pushed = push(firsts, firsts, motion_sems, 1)
    first_pushed.wait_recv()
    for turn in (2, 1, 3):
        line = motion.at[:, y, upper]
        push_to(line, line, relay_sems, region, along_y(turn)).start()
        line = motion.at[x, :, lower]
        push_to(line, line, relay_sems, region, along_x(turn)).start()
    seconds = motion.at[pl.ds(0, 3)]
    second_pushed = push(seconds, seconds, relay_sems, 1)

    @pl.loop(0, panels // 16)
    def _(i):
        base = pl.multiple_of(i * 16, 16)
        lanes = lax.broadcasted_iota(jnp.int32, (16, 128), 1).astype(F32).astype(BF16)
        for k in range(4):
            low = jnp.broadcast_to(column_of[pl.ds(base, 16), k : k + 1], (16, 128)).astype(BF16)
            holder = jnp.broadcast_to(column_of[pl.ds(base, 16), k + 4 : k + 5], (16, 128)).astype(BF16)
            found = jnp.where(low == lanes, one, zero)
            for m in range(members):
                hot_turned[pl.ds(k * panels + base, 16), m * 128 : (m + 1) * 128] = jnp.where(
                    holder == float(m), found, zero
                )

    for g in range(clusters // 2):
        pair = jnp.concatenate([basis_v[2 * g], basis_v[2 * g + 1]], axis=1)
        basis_v_wide[:, g * 128 : (g + 1) * 128] = jnp.concatenate([pair] * loads, axis=0)
    basis_u_high[...] = jnp.zeros_like(basis_u_high)
    basis_u_low[...] = jnp.zeros_like(basis_u_low)
    empty = jnp.zeros((16, block), F32)
    for t in range(clusters):
        parts = [basis_u[t], empty] if t % 2 == 0 else [empty, basis_u[t]]
        high, low = split(jnp.concatenate(parts, axis=1))
        where = (slice(t * 16, t * 16 + 16), slice(t // 2 * 128, t // 2 * 128 + 128))
        basis_u_high[where] = high
        basis_u_low[where] = low
    coup_load.wait()

    @pl.loop(0, clusters)
    def _(t):
        high, low = split(coupling[t].reshape(256, 32))
        coup_cat[t] = jnp.concatenate([high, low], axis=1)

    table[table.shape[0] - 1] = jnp.zeros((8, 128), F32)

    second_pushed.wait_recv()
    for m in range(members):
        motion_cat[:, m * 128 : (m + 1) * 128] = motion[m // 4, m % 4]
    own_rows = pl.ds(pl.multiple_of(me * 128, 128), 128)

    for c in range(3):
        moved[c] = jnp.zeros((8, panels), F32)

    @pl.loop(0, 4)
    def _(k):
        columns = pl.ds(pl.multiple_of(k * panels, panels), panels)
        rows = dot(motion_cat[...], hot[:, columns]) + dot(motion_low[...], hot[own_rows, columns])
        lo = (nodes[pl.ds(k, 1), :] >> 7) & 7
        for c in range(3):
            total = moved[c]
            for q in range(8):
                at = (q * 3 + c) * 8
                total = total + jnp.where(jnp.broadcast_to(lo == q, (8, panels)), rows[at : at + 8], 0.0)
            moved[c] = total

    normal_vel = 0.25 * (
        moved[0] * normals[0:1, :] + moved[1] * normals[1:2, :] + moved[2] * normals[2:3, :]
    )
    density = normal_vel.astype(BF16).astype(F32)
    half = panels // 2
    dens[me] = jnp.concatenate([density[:, :half], density[:, half:]], axis=0).astype(BF16)
    push_all(dens, dens_sems)

    lane_cluster = lax.broadcasted_iota(jnp.int32, (8, panels), 1) // block
    diagonal = jnp.concatenate(
        [jnp.where(lane_cluster == t, density, 0.0) for t in range(clusters)], axis=0
    ).astype(BF16)
    wide = dot_nt(diagonal, basis_v_wide[...])
    row_load = lax.broadcasted_iota(jnp.int32, (128, 128), 0) & 7
    lane_load = lax.broadcasted_iota(jnp.int32, (128, 128), 1) >> 4
    wide = jnp.where(row_load == lane_load, wide, 0.0)
    device = (core * (regions // 2) + plane) * members + me
    coeffs[device] = jnp.sum(wide.reshape(clusters, 8, 128), axis=1).astype(BF16)
    pl.semaphore_wait(ready, regions - 1)
    chips = regions // 2 * members

    @pl.loop(1, chips)
    def _(step):
        there = lax.rem(plane + step // members, regions // 2) * 2 + core
        push_to(coeffs.at[device], coeffs.at[device], coeff_sems, there, member_at(lax.rem(step, members))).start()

    near_load.wait()
    pushed(dens, dens_sems).wait_recv()
    left = lax.broadcasted_iota(jnp.int32, (8, 128), 1) < block

    @pl.loop(0, members)
    def _(m):
        rows = dens[m].astype(F32)
        for h in range(2):
            for g in range(half // 128):
                both = rows[h * 8 : h * 8 + 8, g * 128 : (g + 1) * 128]
                turned = pltpu.roll(both, block, axis=1)
                at = m * clusters + h * (clusters // 2) + g * 2
                table[at] = jnp.where(left, both, turned)
                table[at + 1] = jnp.where(left, turned, both)

    slots = near_cols.shape[1]
    unused = table.shape[0] - 1

    def near_pair(g):
        picked = []
        for h in range(2):
            t = 2 * g + h
            count = near_count[t]
            parts = []
            for j in range(0, slots, 2):
                first = jnp.where(j < count, near_cols[t, j], unused)
                second = jnp.where(j + 1 < count, near_cols[t, j + 1], unused)
                parts.append(jnp.where(left, table[first], table[second]))
            picked.append(jnp.concatenate(parts, axis=1))
        both = jnp.concatenate(picked, axis=0).astype(BF16)
        blocks = near[pl.ds(2 * g, 2)].reshape(2 * block, slots * block)
        result = dot_nt(both, blocks)
        near_pot[:, pl.ds(pl.multiple_of(g * 128, 128), 128)] = jnp.where(left, result[:8], result[8:])

    pl.loop(0, clusters // 4)(near_pair)

    coeff_part = coeffs.at[pl.ds(0, chips - 1)]
    coeff_pushed = push(coeff_part, coeff_part, coeff_sems, 1)
    coeff_pushed.wait_recv()
    side = coeffs.at[pl.ds(pl.multiple_of(core * chips, chips), chips)]
    side_pushed = push_to(side, side, side_sems, region + 1 - 2 * core, me)
    side_pushed.start()
    pl.loop(clusters // 4, clusters // 2)(near_pair)

    side_pushed.wait_recv()

    @pl.loop(0, members)
    def _(i):
        for r in range(regions):
            at = pl.multiple_of((r * members + i) * clusters, clusters)
            d = (r % 2 * (regions // 2) + r // 2) * members + i
            coeff_rows[pl.ds(at, clusters), :] = coeffs[d].astype(F32)

    own_q = lax.broadcasted_iota(jnp.int32, (256, 128), 0) & 15
    lane_q = lax.broadcasted_iota(jnp.int32, (256, 128), 1) & 15
    same_q = own_q == lane_q

    @pl.loop(0, clusters)
    def _(t):
        for a in range(32):
            picked_rows[pl.ds(t * 32 + a, 1), :] = coeff_rows[pl.ds(far_cols[t, a], 1), :]

    for t in range(clusters):
        rows = picked_rows[t * 32 : t * 32 + 32].astype(BF16)
        product = dot(coup_cat[t], jnp.concatenate([rows, rows], axis=0))
        product = jnp.where(same_q, product, 0.0)
        folded[t * 16 : t * 16 + 16] = jnp.sum(product.reshape(16, 16, 128), axis=1)

    fold = jnp.where(
        lax.broadcasted_iota(jnp.int32, (8, 128), 0)
        == lax.broadcasted_iota(jnp.int32, (8, 128), 1) >> 4,
        1.0,
        0.0,
    )
    fold = jnp.concatenate([fold, fold], axis=0).astype(BF16)
    folded_high, folded_low = split(folded[...])
    far_coef = (dot_nt(fold, folded_high) + dot_nt(fold, folded_low))[:8]
    far_high, far_low = split(far_coef)
    far_both = jnp.concatenate([far_high.astype(F32), far_low.astype(F32)], axis=0).astype(BF16)
    with_high = dot(far_both, basis_u_high[...])
    with_low = dot(far_both, basis_u_low[...])
    potential = near_pot[...] + (with_high[:8] + with_high[8:] + with_low[:8])

    scaled = -0.25 * areas[...]
    for c in range(3):
        moved[c] = potential * (scaled * normals[c : c + 1, :])

    @pl.loop(0, panels // 256)
    def _(i):
        base = pl.multiple_of(i * 256, 256)
        load = [moved[c, :, pl.ds(base, 256)] for c in range(3)]
        for k in range(4):
            lo = (nodes[k : k + 1, pl.ds(base, 256)] >> 7) & 7
            rows = []
            for q in range(8):
                hit = jnp.broadcast_to(lo == q, (8, 256))
                rows += [jnp.where(hit, load[c], 0.0) for c in range(3)]
            high, low = split(jnp.concatenate(rows, axis=0))
            columns = pl.ds(k * panels + base, 256)
            spread[0, :, columns] = high
            spread[1, :, columns] = low

    @pl.loop(0, 5)
    def _(i):
        columns = pl.ds(pl.multiple_of((i - i // 4) * 512, 512), 512)
        sums = dot(spread[i // 4], hot_turned[:, columns])

        @pl.when(i < 4)
        def _():
            for h in range(4):
                ahead = lax.rem(h + i + 1, 4)
                to_x, to_y = lax.rem(x + h, 4), lax.rem(y + ahead, 4)
                at = i * 4 + h
                sums_of = sums[:, h * 128 : (h + 1) * 128]
                force_out[at] = sums_of.astype(BF16)
                if h == 0:
                    upper_own[to_y] = sums_of[:half_rows]
                else:
                    push_to(
                        force_out.at[at, upper], upper_in.at[x, to_y], force_sems, region, to_x * 4 + y
                    ).start()

                @pl.when(ahead == 0)
                def _():
                    lower_own[to_x] = sums_of[half_rows:]

                @pl.when(ahead != 0)
                def _():
                    push_to(
                        force_out.at[at, lower], lower_in.at[y, to_x], force_sems, region, x * 4 + to_y
                    ).start()

        @pl.when(i == 4)
        def _():
            upper_own[y] += sums[:half_rows, :128]
            lower_own[x] += sums[half_rows:, :128]

    partial = force_out.at[pl.ds(0, 12)]
    partial_pushed = push(partial, partial, force_sems, 1)
    partial_pushed.wait_recv()

    def upper_sum(to_y):
        total = upper_own[to_y]
        for turn in range(1, 4):
            total = total + upper_in[lax.rem(x + turn, 4), to_y].astype(F32)
        return total

    def lower_sum(to_x):
        total = lower_own[to_x]
        for turn in range(1, 4):
            total = total + lower_in[lax.rem(y + turn, 4), to_x].astype(F32)
        return total

    for turn in (2, 1, 3):
        last_out[turn, upper] = upper_sum(lax.rem(y + turn, 4)).astype(BF16)
        piece = (last_out.at[turn, upper], last_in.at[turn, upper])
        push_to(*piece, last_sems, region, along_y(turn)).start()
        last_out[turn, lower] = lower_sum(lax.rem(x + turn, 4)).astype(BF16)
        piece = (last_out.at[turn, lower], last_in.at[turn, lower])
        push_to(*piece, last_sems, region, along_x(turn)).start()
    total = jnp.concatenate([upper_sum(y), lower_sum(x)], axis=0)
    last = last_out.at[pl.ds(1, 3)]
    last_pushed = push(last, last, last_sems, 1)
    last_pushed.wait_recv()
    for turn in range(1, 4):
        total = total + last_in[turn].astype(F32)
    for lo in range(8):
        for c in range(3):
            at = (lo * 3 + c) * 8
            out[c, :, lo * 128 : (lo + 1) * 128] = total[at : at + 8]

    first_pushed.wait_send()
    second_pushed.wait_send()
    pushed(dens, dens_sems).wait_send()
    coeff_pushed.wait_send()
    side_pushed.wait_send()
    partial_pushed.wait_send()
    last_pushed.wait_send()


def push_to(source, target, sems, region, member):
    return pltpu.make_async_remote_copy(
        src_ref=source,
        dst_ref=target,
        send_sem=sems.at[0],
        recv_sem=sems.at[1],
        device_id=(region, member),
        device_id_type=MESH,
    )


def body(
    regions,
    members,
    velocity,
    normals,
    areas,
    panel_nodes,
    near_blocks,
    near_cols,
    near_count,
    basis_v,
    basis_u,
    coupling,
    far_cols,
):
    nodes = velocity.shape[2]
    panels = normals.shape[1]
    clusters, block = near_blocks.shape[0], near_blocks.shape[1]
    rows = 24 * nodes // 128
    lanes = members * 128
    smem = pl.BlockSpec(memory_space=pltpu.SMEM)
    vmem = pl.BlockSpec(memory_space=pltpu.VMEM)
    hbm = pl.BlockSpec(memory_space=pl.ANY)
    dma = pltpu.SemaphoreType.DMA
    result = pl.pallas_call(
        functools.partial(kernel, regions, members),
        out_shape=jax.ShapeDtypeStruct((3, 8, nodes), F32),
        in_specs=[smem] * 3 + [vmem] * 6 + [hbm] * 2,
        out_specs=vmem,
        scratch_shapes=[
            pltpu.VMEM(near_blocks.shape, BF16),
            pltpu.VMEM((clusters, 16, 16, 32), F32),
            pltpu.VMEM((lanes, 4 * panels), BF16),
            pltpu.VMEM((4 * panels, lanes), BF16),
            pltpu.VMEM((panels, 8), F32),
            pltpu.VMEM((4, 4, rows, 128), BF16),
            pltpu.VMEM((rows, lanes), BF16),
            pltpu.VMEM((rows, 128), BF16),
            pltpu.VMEM((3, 8, panels), F32),
            pltpu.VMEM((members, 16, panels // 2), BF16),
            pltpu.VMEM((members * clusters + 1, 8, 128), F32),
            pltpu.VMEM((members * regions, clusters, 128), BF16),
            pltpu.VMEM((members * regions * clusters, 128), F32),
            pltpu.VMEM((clusters * 32, 128), F32),
            pltpu.VMEM((clusters, 256, 64), BF16),
            pltpu.VMEM((clusters * 16, 128), F32),
            pltpu.VMEM((128, panels), BF16),
            pltpu.VMEM((clusters * 16, panels), BF16),
            pltpu.VMEM((clusters * 16, panels), BF16),
            pltpu.VMEM((8, panels), F32),
            pltpu.VMEM((2, rows, 4 * panels), BF16),
            pltpu.VMEM((members, rows, 128), BF16),
            pltpu.VMEM((4, rows // 2, 128), F32),
            pltpu.VMEM((4, rows // 2, 128), F32),
            pltpu.VMEM((4, 4, rows // 2, 128), BF16),
            pltpu.VMEM((4, 4, rows // 2, 128), BF16),
            pltpu.VMEM((4, rows, 128), BF16),
            pltpu.VMEM((4, rows, 128), BF16),
            dma((2,)),
            dma((2,)),
            dma((2,)),
            dma((2,)),
            dma((2,)),
            dma((2,)),
            dma((2,)),
            dma((2,)),
            pltpu.SemaphoreType.REGULAR,
        ],
        compiler_params=pltpu.CompilerParams(
            collective_id=0, has_side_effects=True, vmem_limit_bytes=56 * 1024 * 1024
        ),
        name="hull",
    )(
        near_cols,
        near_count,
        far_cols,
        jnp.transpose(velocity, (1, 0, 2)),
        normals,
        areas.reshape(1, panels),
        panel_nodes.T,
        jnp.transpose(basis_v, (0, 2, 1)),
        jnp.transpose(basis_u, (0, 2, 1)),
        near_blocks,
        jnp.transpose(coupling, (0, 2, 3, 1)),
    )
    return jnp.transpose(result, (1, 0, 2))


def solution(mesh):
    both = ("region", "member")
    placed = (
        P(None, None, both),
        P(None, both),
        P(both),
        P(both, None),
        P(both, None, None),
        P(both, None),
        P(both),
        P(both, None, None),
        P(both, None, None),
        P(both, None, None, None),
        P(both, None),
    )
    return jax.shard_map(
        functools.partial(body, mesh.shape["region"], mesh.shape["member"]),
        mesh=mesh,
        in_specs=placed,
        out_specs=P(None, None, both),
        check_vma=False,
    )
```

```python
import functools

import jax
import jax.numpy as jnp
from jax import lax
from jax.experimental import pallas as pl
from jax.experimental.pallas import tpu as pltpu
from jax.sharding import PartitionSpec as P

MESH = pl.DeviceIdType.MESH
F32 = jnp.float32
BF16 = jnp.bfloat16
NT = (((1,), (1,)), ((), ()))


def split(x):
    high = x.astype(BF16)
    return high, (x - high.astype(F32)).astype(BF16)


def dot(a, b):
    return jnp.dot(a, b, preferred_element_type=F32)


def dot_nt(a, b):
    return lax.dot_general(a, b, NT, preferred_element_type=F32)


def kernel(
    regions,
    members,
    near_cols_hbm,
    near_count_hbm,
    far_cols_hbm,
    velocity_hbm,
    normals_hbm,
    areas_hbm,
    nodes_hbm,
    basis_v_hbm,
    basis_u_hbm,
    near_hbm,
    coupling_hbm,
    out,
    near_cols,
    near_count,
    far_cols,
    velocity,
    normals,
    areas,
    nodes,
    basis_v,
    basis_u,
    near,
    coupling,
    hot,
    hot_turned,
    column_of,
    motion,
    motion_cat,
    motion_low,
    moved,
    dens,
    table,
    coeffs,
    coeff_rows,
    picked_rows,
    coup_cat,
    folded,
    basis_v_wide,
    basis_u_high,
    basis_u_low,
    near_pot,
    spread,
    force_out,
    upper_own,
    lower_own,
    upper_in,
    lower_in,
    last_out,
    last_in,
    load_sems,
    motion_sems,
    relay_sems,
    dens_sems,
    coeff_sems,
    side_sems,
    force_sems,
    last_sems,
    ready,
):
    region = lax.axis_index("region")
    me = lax.axis_index("member")
    x, y = me // 4, lax.rem(me, 4)
    plane, core = region // 2, lax.rem(region, 2)
    clusters, block = near.shape[0], near.shape[1]
    panels = nodes.shape[1]
    loads = velocity.shape[1]

    def member_at(step):
        return lax.rem(me + step, members)

    def load(source, target, at):
        return pltpu.make_async_copy(source, target, load_sems.at[at])

    velocity_load = load(velocity_hbm, velocity, 0)
    nodes_load = load(nodes_hbm, nodes, 1)
    near_load = load(near_hbm, near, 2)
    coup_load = load(coupling_hbm, coupling, 3)
    small_loads = [
        load(normals_hbm, normals, 4),
        load(areas_hbm, areas, 5),
        load(basis_v_hbm, basis_v, 6),
        load(basis_u_hbm, basis_u, 7),
        load(near_cols_hbm, near_cols, 8),
        load(near_count_hbm, near_count, 9),
        load(far_cols_hbm, far_cols, 10),
    ]
    velocity_load.start()
    barrier = pltpu.get_barrier_semaphore()
    for step in range(1, members):
        pl.semaphore_signal(barrier, inc=1, device_id=(region, member_at(step)), device_id_type=MESH)
    for step in range(1, regions):
        pl.semaphore_signal(
            barrier, inc=1, device_id=(lax.rem(region + step, regions), me), device_id_type=MESH
        )

    nodes_load.start()
    near_load.start()
    coup_load.start()
    for copy in small_loads:
        copy.start()

    def push(source, target, sems, step):
        return push_to(source, target, sems, region, member_at(step))

    def push_all(rows, sems):
        @pl.loop(1, members)
        def _(step):
            push(rows.at[me], rows.at[me], sems, step).start()

    def pushed(rows, sems):
        part = rows.at[pl.ds(0, members - 1)]
        return push(part, part, sems, 1)

    velocity_load.wait()
    own = jnp.concatenate(
        [velocity[c, :, lo * 128 : (lo + 1) * 128] for lo in range(8) for c in range(3)], axis=0
    )
    own_high, own_low = split(own)
    motion[x, y] = own_high
    motion_low[...] = own_low
    pl.semaphore_wait(barrier, members - 1 + regions - 1)
    half_rows = motion.shape[2] // 2
    upper, lower = pl.ds(0, half_rows), pl.ds(half_rows, half_rows)

    def along_x(turn):
        return lax.rem(x + turn, 4) * 4 + y

    def along_y(turn):
        return x * 4 + lax.rem(y + turn, 4)

    for turn in (2, 1, 3):
        mine = motion.at[x, y, upper]
        push_to(mine, mine, motion_sems, region, along_x(turn)).start()
        mine = motion.at[x, y, lower]
        push_to(mine, mine, motion_sems, region, along_y(turn)).start()
    for step in range(1, regions):
        pl.semaphore_signal(
            ready, inc=1, device_id=(lax.rem(region + step, regions), me), device_id_type=MESH
        )

    nodes_load.wait()
    node = nodes[...]
    lanes_low, owner = (node & 127).astype(F32), (node >> 10).astype(F32)
    ahead_x = ((node >> 12) - x) & 3
    ahead_y = (((node >> 10) & 3) - y) & 3
    stand = (((ahead_y - ahead_x + 3) & 3) * 4 + ahead_x).astype(F32)
    column_of[...] = jnp.transpose(jnp.concatenate([lanes_low, stand], axis=0))
    one, zero = jnp.ones((), BF16), jnp.zeros((), BF16)

    @pl.loop(0, 8)
    def _(i):
        base = pl.multiple_of(i * 16, 16)
        rows = (lax.broadcasted_iota(jnp.int32, (16, panels), 0) + base).astype(F32).astype(BF16)
        for k in range(4):
            low = jnp.broadcast_to(lanes_low[k : k + 1], (16, panels)).astype(BF16)
            holder = jnp.broadcast_to(owner[k : k + 1], (16, panels)).astype(BF16)
            found = jnp.where(low == rows, one, zero)
            for m in range(members):
                hot[pl.ds(m * 128 + base, 16), k * panels : (k + 1) * panels] = jnp.where(
                    holder == float(m), found, zero
                )

    firsts = motion.at[0, pl.ds(0, 3)]
    first_pushed = push(firsts, firsts, motion_sems, 1)
    first_pushed.wait_recv()
    for turn in (2, 1, 3):
        line = motion.at[:, y, upper]
        push_to(line, line, relay_sems, region, along_y(turn)).start()
        line = motion.at[x, :, lower]
        push_to(line, line, relay_sems, region, along_x(turn)).start()
    seconds = motion.at[pl.ds(0, 3)]
    second_pushed = push(seconds, seconds, relay_sems, 1)

    @pl.loop(0, panels // 16)
    def _(i):
        base = pl.multiple_of(i * 16, 16)
        lanes = lax.broadcasted_iota(jnp.int32, (16, 128), 1).astype(F32).astype(BF16)
        for k in range(4):
            low = jnp.broadcast_to(column_of[pl.ds(base, 16), k : k + 1], (16, 128)).astype(BF16)
            holder = jnp.broadcast_to(column_of[pl.ds(base, 16), k + 4 : k + 5], (16, 128)).astype(BF16)
            found = jnp.where(low == lanes, one, zero)
            for m in range(members):
                hot_turned[pl.ds(k * panels + base, 16), m * 128 : (m + 1) * 128] = jnp.where(
                    holder == float(m), found, zero
                )

    for copy in small_loads:
        copy.wait()
    for g in range(clusters // 2):
        pair = jnp.concatenate([basis_v[2 * g], basis_v[2 * g + 1]], axis=1)
        basis_v_wide[:, g * 128 : (g + 1) * 128] = jnp.concatenate([pair] * loads, axis=0)
    basis_u_high[...] = jnp.zeros_like(basis_u_high)
    basis_u_low[...] = jnp.zeros_like(basis_u_low)
    empty = jnp.zeros((16, block), F32)
    for t in range(clusters):
        parts = [basis_u[t], empty] if t % 2 == 0 else [empty, basis_u[t]]
        high, low = split(jnp.concatenate(parts, axis=1))
        where = (slice(t * 16, t * 16 + 16), slice(t // 2 * 128, t // 2 * 128 + 128))
        basis_u_high[where] = high
        basis_u_low[where] = low
    coup_load.wait()

    @pl.loop(0, clusters)
    def _(t):
        high, low = split(coupling[t].reshape(256, 32))
        coup_cat[t] = jnp.concatenate([high, low], axis=1)

    table[table.shape[0] - 1] = jnp.zeros((8, 128), F32)

    second_pushed.wait_recv()
    for m in range(members):
        motion_cat[:, m * 128 : (m + 1) * 128] = motion[m // 4, m % 4]
    own_rows = pl.ds(pl.multiple_of(me * 128, 128), 128)

    for c in range(3):
        moved[c] = jnp.zeros((8, panels), F32)

    @pl.loop(0, 4)
    def _(k):
        columns = pl.ds(pl.multiple_of(k * panels, panels), panels)
        rows = dot(motion_cat[...], hot[:, columns]) + dot(motion_low[...], hot[own_rows, columns])
        lo = (nodes[pl.ds(k, 1), :] >> 7) & 7
        for c in range(3):
            total = moved[c]
            for q in range(8):
                at = (q * 3 + c) * 8
                total = total + jnp.where(jnp.broadcast_to(lo == q, (8, panels)), rows[at : at + 8], 0.0)
            moved[c] = total

    normal_vel = 0.25 * (
        moved[0] * normals[0:1, :] + moved[1] * normals[1:2, :] + moved[2] * normals[2:3, :]
    )
    density = normal_vel.astype(BF16).astype(F32)
    half = panels // 2
    dens[me] = jnp.concatenate([density[:, :half], density[:, half:]], axis=0).astype(BF16)
    lane_cluster = lax.broadcasted_iota(jnp.int32, (8, panels), 1) // block
    diagonal = jnp.concatenate(
        [jnp.where(lane_cluster == t, density, 0.0) for t in range(clusters)], axis=0
    ).astype(BF16)
    wide = dot_nt(diagonal, basis_v_wide[...])
    row_load = lax.broadcasted_iota(jnp.int32, (128, 128), 0) & 7
    lane_load = lax.broadcasted_iota(jnp.int32, (128, 128), 1) >> 4
    wide = jnp.where(row_load == lane_load, wide, 0.0)
    device = (core * (regions // 2) + plane) * members + me
    coeffs[device] = jnp.sum(wide.reshape(clusters, 8, 128), axis=1).astype(BF16)
    pl.semaphore_wait(ready, regions - 1)
    chips = regions // 2 * members

    @pl.loop(1, chips)
    def _(step):
        there = lax.rem(plane + step // members, regions // 2) * 2 + core
        push_to(coeffs.at[device], coeffs.at[device], coeff_sems, there, member_at(lax.rem(step, members))).start()

    push_all(dens, dens_sems)

    coeff_part = coeffs.at[pl.ds(0, chips - 1)]
    coeff_pushed = push(coeff_part, coeff_part, coeff_sems, 1)
    coeff_pushed.wait_recv()
    side = coeffs.at[pl.ds(pl.multiple_of(core * chips, chips), chips)]
    side_pushed = push_to(side, side, side_sems, region + 1 - 2 * core, me)
    side_pushed.start()
    near_load.wait()
    pushed(dens, dens_sems).wait_recv()
    left = lax.broadcasted_iota(jnp.int32, (8, 128), 1) < block

    @pl.loop(0, members)
    def _(m):
        rows = dens[m].astype(F32)
        for h in range(2):
            for g in range(half // 128):
                both = rows[h * 8 : h * 8 + 8, g * 128 : (g + 1) * 128]
                turned = pltpu.roll(both, block, axis=1)
                at = m * clusters + h * (clusters // 2) + g * 2
                table[at] = jnp.where(left, both, turned)
                table[at + 1] = jnp.where(left, turned, both)

    slots = near_cols.shape[1]
    unused = table.shape[0] - 1

    def near_pair(g):
        picked = []
        for h in range(2):
            t = 2 * g + h
            count = near_count[t]
            parts = []
            for j in range(0, slots, 2):
                first = jnp.where(j < count, near_cols[t, j], unused)
                second = jnp.where(j + 1 < count, near_cols[t, j + 1], unused)
                parts.append(jnp.where(left, table[first], table[second]))
            picked.append(jnp.concatenate(parts, axis=1))
        both = jnp.concatenate(picked, axis=0).astype(BF16)
        blocks = near[pl.ds(2 * g, 2)].reshape(2 * block, slots * block)
        result = dot_nt(both, blocks)
        near_pot[:, pl.ds(pl.multiple_of(g * 128, 128), 128)] = jnp.where(left, result[:8], result[8:])

    @pl.loop(0, clusters // 2, unroll=4)
    def _(g):
        near_pair(g)

    side_pushed.wait_recv()

    @pl.loop(0, members)
    def _(i):
        for r in range(regions):
            at = pl.multiple_of((r * members + i) * clusters, clusters)
            d = (r % 2 * (regions // 2) + r // 2) * members + i
            coeff_rows[pl.ds(at, clusters), :] = coeffs[d].astype(F32)

    own_q = lax.broadcasted_iota(jnp.int32, (256, 128), 0) & 15
    lane_q = lax.broadcasted_iota(jnp.int32, (256, 128), 1) & 15
    same_q = own_q == lane_q

    @pl.loop(0, clusters)
    def _(t):
        for a in range(32):
            picked_rows[pl.ds(t * 32 + a, 1), :] = coeff_rows[pl.ds(far_cols[t, a], 1), :]

    for t in range(clusters):
        rows = picked_rows[t * 32 : t * 32 + 32].astype(BF16)
        product = dot(coup_cat[t], jnp.concatenate([rows, rows], axis=0))
        product = jnp.where(same_q, product, 0.0)
        folded[t * 16 : t * 16 + 16] = jnp.sum(product.reshape(16, 16, 128), axis=1)

    fold = jnp.where(
        lax.broadcasted_iota(jnp.int32, (8, 128), 0)
        == lax.broadcasted_iota(jnp.int32, (8, 128), 1) >> 4,
        1.0,
        0.0,
    )
    fold = jnp.concatenate([fold, fold], axis=0).astype(BF16)
    folded_high, folded_low = split(folded[...])
    far_coef = (dot_nt(fold, folded_high) + dot_nt(fold, folded_low))[:8]
    far_high, far_low = split(far_coef)
    far_both = jnp.concatenate([far_high.astype(F32), far_low.astype(F32)], axis=0).astype(BF16)
    with_high = dot(far_both, basis_u_high[...])
    with_low = dot(far_both, basis_u_low[...])
    potential = near_pot[...] + (with_high[:8] + with_high[8:] + with_low[:8])

    scaled = -0.25 * areas[...]
    for c in range(3):
        moved[c] = potential * (scaled * normals[c : c + 1, :])

    @pl.loop(0, panels // 256)
    def _(i):
        base = pl.multiple_of(i * 256, 256)
        load = [moved[c, :, pl.ds(base, 256)] for c in range(3)]
        for k in range(4):
            lo = (nodes[k : k + 1, pl.ds(base, 256)] >> 7) & 7
            rows = []
            for q in range(8):
                hit = jnp.broadcast_to(lo == q, (8, 256))
                rows += [jnp.where(hit, load[c], 0.0) for c in range(3)]
            high, low = split(jnp.concatenate(rows, axis=0))
            columns = pl.ds(k * panels + base, 256)
            spread[0, :, columns] = high
            spread[1, :, columns] = low

    @pl.loop(0, 5)
    def _(i):
        columns = pl.ds(pl.multiple_of((i - i // 4) * 512, 512), 512)
        sums = dot(spread[i // 4], hot_turned[:, columns])

        @pl.when(i < 4)
        def _():
            for h in range(4):
                ahead = lax.rem(h + i + 1, 4)
                to_x, to_y = lax.rem(x + h, 4), lax.rem(y + ahead, 4)
                at = i * 4 + h
                sums_of = sums[:, h * 128 : (h + 1) * 128]
                force_out[at] = sums_of.astype(BF16)
                if h == 0:
                    upper_own[to_y] = sums_of[:half_rows]
                else:
                    push_to(
                        force_out.at[at, upper], upper_in.at[x, to_y], force_sems, region, to_x * 4 + y
                    ).start()

                @pl.when(ahead == 0)
                def _():
                    lower_own[to_x] = sums_of[half_rows:]

                @pl.when(ahead != 0)
                def _():
                    push_to(
                        force_out.at[at, lower], lower_in.at[y, to_x], force_sems, region, x * 4 + to_y
                    ).start()

        @pl.when(i == 4)
        def _():
            upper_own[y] += sums[:half_rows, :128]
            lower_own[x] += sums[half_rows:, :128]

    partial = force_out.at[pl.ds(0, 12)]
    partial_pushed = push(partial, partial, force_sems, 1)
    partial_pushed.wait_recv()

    def upper_sum(to_y):
        total = upper_own[to_y]
        for turn in range(1, 4):
            total = total + upper_in[lax.rem(x + turn, 4), to_y].astype(F32)
        return total

    def lower_sum(to_x):
        total = lower_own[to_x]
        for turn in range(1, 4):
            total = total + lower_in[lax.rem(y + turn, 4), to_x].astype(F32)
        return total

    for turn in (2, 1, 3):
        last_out[turn, upper] = upper_sum(lax.rem(y + turn, 4)).astype(BF16)
        piece = (last_out.at[turn, upper], last_in.at[turn, upper])
        push_to(*piece, last_sems, region, along_y(turn)).start()
        last_out[turn, lower] = lower_sum(lax.rem(x + turn, 4)).astype(BF16)
        piece = (last_out.at[turn, lower], last_in.at[turn, lower])
        push_to(*piece, last_sems, region, along_x(turn)).start()
    total = jnp.concatenate([upper_sum(y), lower_sum(x)], axis=0)
    last = last_out.at[pl.ds(1, 3)]
    last_pushed = push(last, last, last_sems, 1)
    last_pushed.wait_recv()
    for turn in range(1, 4):
        total = total + last_in[turn].astype(F32)
    for lo in range(8):
        for c in range(3):
            at = (lo * 3 + c) * 8
            out[c, :, lo * 128 : (lo + 1) * 128] = total[at : at + 8]

    first_pushed.wait_send()
    second_pushed.wait_send()
    pushed(dens, dens_sems).wait_send()
    coeff_pushed.wait_send()
    side_pushed.wait_send()
    partial_pushed.wait_send()
    last_pushed.wait_send()


def push_to(source, target, sems, region, member):
    return pltpu.make_async_remote_copy(
        src_ref=source,
        dst_ref=target,
        send_sem=sems.at[0],
        recv_sem=sems.at[1],
        device_id=(region, member),
        device_id_type=MESH,
    )


def body(
    regions,
    members,
    velocity,
    normals,
    areas,
    panel_nodes,
    near_blocks,
    near_cols,
    near_count,
    basis_v,
    basis_u,
    coupling,
    far_cols,
):
    nodes = velocity.shape[2]
    panels = normals.shape[1]
    clusters, block = near_blocks.shape[0], near_blocks.shape[1]
    rows = 24 * nodes // 128
    lanes = members * 128
    vmem = pl.BlockSpec(memory_space=pltpu.VMEM)
    hbm = pl.BlockSpec(memory_space=pl.ANY)
    dma = pltpu.SemaphoreType.DMA
    result = pl.pallas_call(
        functools.partial(kernel, regions, members),
        out_shape=pltpu.VMEM((3, 8, nodes), F32),
        in_specs=[hbm] * 11,
        out_specs=vmem,
        scratch_shapes=[
            pltpu.SMEM(near_cols.shape, jnp.int32),
            pltpu.SMEM(near_count.shape, jnp.int32),
            pltpu.SMEM(far_cols.shape, jnp.int32),
            pltpu.VMEM((3, 8, nodes), F32),
            pltpu.VMEM(normals.shape, F32),
            pltpu.VMEM((1, panels), F32),
            pltpu.VMEM((4, panels), jnp.int32),
            pltpu.VMEM((clusters, 16, block), BF16),
            pltpu.VMEM((clusters, 16, block), F32),
            pltpu.VMEM(near_blocks.shape, BF16),
            pltpu.VMEM((clusters, 16, 16, 32), F32),
            pltpu.VMEM((lanes, 4 * panels), BF16),
            pltpu.VMEM((4 * panels, lanes), BF16),
            pltpu.VMEM((panels, 8), F32),
            pltpu.VMEM((4, 4, rows, 128), BF16),
            pltpu.VMEM((rows, lanes), BF16),
            pltpu.VMEM((rows, 128), BF16),
            pltpu.VMEM((3, 8, panels), F32),
            pltpu.VMEM((members, 16, panels // 2), BF16),
            pltpu.VMEM((members * clusters + 1, 8, 128), F32),
            pltpu.VMEM((members * regions, clusters, 128), BF16),
            pltpu.VMEM((members * regions * clusters, 128), F32),
            pltpu.VMEM((clusters * 32, 128), F32),
            pltpu.VMEM((clusters, 256, 64), BF16),
            pltpu.VMEM((clusters * 16, 128), F32),
            pltpu.VMEM((128, panels), BF16),
            pltpu.VMEM((clusters * 16, panels), BF16),
            pltpu.VMEM((clusters * 16, panels), BF16),
            pltpu.VMEM((8, panels), F32),
            pltpu.VMEM((2, rows, 4 * panels), BF16),
            pltpu.VMEM((members, rows, 128), BF16),
            pltpu.VMEM((4, rows // 2, 128), F32),
            pltpu.VMEM((4, rows // 2, 128), F32),
            pltpu.VMEM((4, 4, rows // 2, 128), BF16),
            pltpu.VMEM((4, 4, rows // 2, 128), BF16),
            pltpu.VMEM((4, rows, 128), BF16),
            pltpu.VMEM((4, rows, 128), BF16),
            dma((11,)),
            dma((2,)),
            dma((2,)),
            dma((2,)),
            dma((2,)),
            dma((2,)),
            dma((2,)),
            dma((2,)),
            pltpu.SemaphoreType.REGULAR,
        ],
        compiler_params=pltpu.CompilerParams(
            collective_id=0, has_side_effects=True, vmem_limit_bytes=56 * 1024 * 1024
        ),
        name="hull",
    )(
        near_cols,
        near_count,
        far_cols,
        jnp.transpose(velocity, (1, 0, 2)),
        normals,
        areas.reshape(1, panels),
        panel_nodes.T,
        jnp.transpose(basis_v, (0, 2, 1)),
        jnp.transpose(basis_u, (0, 2, 1)),
        near_blocks,
        jnp.transpose(coupling, (0, 2, 3, 1)),
    )
    return jnp.transpose(result, (1, 0, 2))


def solution(mesh):
    both = ("region", "member")
    placed = (
        P(None, None, both),
        P(None, both),
        P(both),
        P(both, None),
        P(both, None, None),
        P(both, None),
        P(both),
        P(both, None, None),
        P(both, None, None),
        P(both, None, None, None),
        P(both, None),
    )
    return jax.shard_map(
        functools.partial(body, mesh.shape["region"], mesh.shape["member"]),
        mesh=mesh,
        in_specs=placed,
        out_specs=P(None, None, both),
        check_vma=False,
    )
```

```python
import functools

import jax
import jax.numpy as jnp
from jax import lax
from jax.experimental import pallas as pl
from jax.experimental.pallas import tpu as pltpu
from jax.sharding import PartitionSpec as P

MESH = pl.DeviceIdType.MESH
F32 = jnp.float32
BF16 = jnp.bfloat16
NT = (((1,), (1,)), ((), ()))


def split(x):
    high = x.astype(BF16)
    return high, (x - high.astype(F32)).astype(BF16)


def dot(a, b):
    return jnp.dot(a, b, preferred_element_type=F32)


def dot_nt(a, b):
    return lax.dot_general(a, b, NT, preferred_element_type=F32)


def kernel(
    regions,
    members,
    near_cols_hbm,
    near_count_hbm,
    far_cols_hbm,
    velocity_hbm,
    normals_hbm,
    areas_hbm,
    nodes_hbm,
    basis_v_hbm,
    basis_u_hbm,
    near_hbm,
    coupling_hbm,
    out,
    near_cols,
    near_count,
    far_cols,
    velocity,
    normals,
    areas,
    nodes,
    basis_v,
    basis_u,
    near,
    coupling,
    hot,
    hot_turned,
    column_of,
    motion,
    motion_cat,
    motion_low,
    moved,
    dens,
    table,
    coeffs,
    coeff_rows,
    picked_rows,
    coup_cat,
    folded,
    basis_v_wide,
    basis_u_high,
    basis_u_low,
    near_pot,
    spread,
    force_out,
    upper_own,
    lower_own,
    upper_in,
    lower_in,
    last_out,
    last_in,
    load_sems,
    motion_sems,
    relay_sems,
    dens_sems,
    coeff_sems,
    side_sems,
    force_sems,
    last_sems,
    ready,
):
    region = lax.axis_index("region")
    me = lax.axis_index("member")
    x, y = me // 4, lax.rem(me, 4)
    plane, core = region // 2, lax.rem(region, 2)
    clusters, block = near.shape[0], near.shape[1]
    panels = nodes.shape[1]
    loads = velocity.shape[1]

    def member_at(step):
        return lax.rem(me + step, members)

    def along_x(turn):
        return lax.rem(x + turn, 4) * 4 + y

    def along_y(turn):
        return x * 4 + lax.rem(y + turn, 4)

    def load(source, target, at):
        return pltpu.make_async_copy(source, target, load_sems.at[at])

    velocity_load = load(velocity_hbm, velocity, 0)
    nodes_load = load(nodes_hbm, nodes, 1)
    near_load = load(near_hbm, near, 2)
    coup_load = load(coupling_hbm, coupling, 3)
    small_loads = [
        load(normals_hbm, normals, 4),
        load(areas_hbm, areas, 5),
        load(basis_v_hbm, basis_v, 6),
        load(basis_u_hbm, basis_u, 7),
        load(near_cols_hbm, near_cols, 8),
        load(near_count_hbm, near_count, 9),
        load(far_cols_hbm, far_cols, 10),
    ]
    velocity_load.start()
    barrier = pltpu.get_barrier_semaphore()
    for turn in range(1, 4):
        for peer in (along_x(turn), along_y(turn)):
            pl.semaphore_signal(barrier, inc=1, device_id=(region, peer), device_id_type=MESH)
    for step in range(1, regions):
        pl.semaphore_signal(
            barrier, inc=1, device_id=(lax.rem(region + step, regions), me), device_id_type=MESH
        )

    nodes_load.start()
    near_load.start()
    coup_load.start()
    for copy in small_loads:
        copy.start()

    def push(source, target, sems, step):
        return push_to(source, target, sems, region, member_at(step))

    def push_all(rows, sems):
        @pl.loop(1, members)
        def _(step):
            push(rows.at[me], rows.at[me], sems, step).start()

    def pushed(rows, sems):
        part = rows.at[pl.ds(0, members - 1)]
        return push(part, part, sems, 1)

    velocity_load.wait()
    own = jnp.concatenate(
        [velocity[c, :, lo * 128 : (lo + 1) * 128] for lo in range(8) for c in range(3)], axis=0
    )
    own_high, own_low = split(own)
    motion[x, y] = own_high
    motion_low[...] = own_low
    pl.semaphore_wait(barrier, 6 + regions - 1)
    half_rows = motion.shape[2] // 2
    upper, lower = pl.ds(0, half_rows), pl.ds(half_rows, half_rows)

    for turn in (2, 1, 3):
        mine = motion.at[x, y, upper]
        push_to(mine, mine, motion_sems, region, along_x(turn)).start()
        mine = motion.at[x, y, lower]
        push_to(mine, mine, motion_sems, region, along_y(turn)).start()

    nodes_load.wait()
    node = nodes[...]
    lanes_low, owner = (node & 127).astype(F32), (node >> 10).astype(F32)
    ahead_x = ((node >> 12) - x) & 3
    ahead_y = (((node >> 10) & 3) - y) & 3
    stand = (((ahead_y - ahead_x + 3) & 3) * 4 + ahead_x).astype(F32)
    column_of[...] = jnp.transpose(jnp.concatenate([lanes_low, stand], axis=0))
    one, zero = jnp.ones((), BF16), jnp.zeros((), BF16)

    @pl.loop(0, 8)
    def _(i):
        base = pl.multiple_of(i * 16, 16)
        rows = (lax.broadcasted_iota(jnp.int32, (16, panels), 0) + base).astype(F32).astype(BF16)
        for k in range(4):
            low = jnp.broadcast_to(lanes_low[k : k + 1], (16, panels)).astype(BF16)
            holder = jnp.broadcast_to(owner[k : k + 1], (16, panels)).astype(BF16)
            found = jnp.where(low == rows, one, zero)
            for m in range(members):
                hot[pl.ds(m * 128 + base, 16), k * panels : (k + 1) * panels] = jnp.where(
                    holder == float(m), found, zero
                )

    firsts = motion.at[0, pl.ds(0, 3)]
    first_pushed = push(firsts, firsts, motion_sems, 1)
    first_pushed.wait_recv()
    for turn in (2, 1, 3):
        line = motion.at[:, y, upper]
        push_to(line, line, relay_sems, region, along_y(turn)).start()
        line = motion.at[x, :, lower]
        push_to(line, line, relay_sems, region, along_x(turn)).start()
    for step in range(1, regions):
        pl.semaphore_signal(
            ready, inc=1, device_id=(lax.rem(region + step, regions), me), device_id_type=MESH
        )
    seconds = motion.at[pl.ds(0, 3)]
    second_pushed = push(seconds, seconds, relay_sems, 1)

    @pl.loop(0, panels // 16)
    def _(i):
        base = pl.multiple_of(i * 16, 16)
        lanes = lax.broadcasted_iota(jnp.int32, (16, 128), 1).astype(F32).astype(BF16)
        for k in range(4):
            low = jnp.broadcast_to(column_of[pl.ds(base, 16), k : k + 1], (16, 128)).astype(BF16)
            holder = jnp.broadcast_to(column_of[pl.ds(base, 16), k + 4 : k + 5], (16, 128)).astype(BF16)
            found = jnp.where(low == lanes, one, zero)
            for m in range(members):
                hot_turned[pl.ds(k * panels + base, 16), m * 128 : (m + 1) * 128] = jnp.where(
                    holder == float(m), found, zero
                )

    for copy in small_loads:
        copy.wait()
    for g in range(clusters // 2):
        pair = jnp.concatenate([basis_v[2 * g], basis_v[2 * g + 1]], axis=1)
        basis_v_wide[:, g * 128 : (g + 1) * 128] = jnp.concatenate([pair] * loads, axis=0)
    basis_u_high[...] = jnp.zeros_like(basis_u_high)
    basis_u_low[...] = jnp.zeros_like(basis_u_low)
    empty = jnp.zeros((16, block), F32)
    for t in range(clusters):
        parts = [basis_u[t], empty] if t % 2 == 0 else [empty, basis_u[t]]
        high, low = split(jnp.concatenate(parts, axis=1))
        where = (slice(t * 16, t * 16 + 16), slice(t // 2 * 128, t // 2 * 128 + 128))
        basis_u_high[where] = high
        basis_u_low[where] = low
    coup_load.wait()

    @pl.loop(0, clusters)
    def _(t):
        high, low = split(coupling[t].reshape(256, 32))
        coup_cat[t] = jnp.concatenate([high, low], axis=1)

    table[table.shape[0] - 1] = jnp.zeros((8, 128), F32)

    second_pushed.wait_recv()
    for m in range(members):
        motion_cat[:, m * 128 : (m + 1) * 128] = motion[m // 4, m % 4]
    own_rows = pl.ds(pl.multiple_of(me * 128, 128), 128)

    for c in range(3):
        moved[c] = jnp.zeros((8, panels), F32)

    @pl.loop(0, 4)
    def _(k):
        columns = pl.ds(pl.multiple_of(k * panels, panels), panels)
        rows = dot(motion_cat[...], hot[:, columns]) + dot(motion_low[...], hot[own_rows, columns])
        lo = (nodes[pl.ds(k, 1), :] >> 7) & 7
        for c in range(3):
            total = moved[c]
            for q in range(8):
                at = (q * 3 + c) * 8
                total = total + jnp.where(jnp.broadcast_to(lo == q, (8, panels)), rows[at : at + 8], 0.0)
            moved[c] = total

    normal_vel = 0.25 * (
        moved[0] * normals[0:1, :] + moved[1] * normals[1:2, :] + moved[2] * normals[2:3, :]
    )
    density = normal_vel.astype(BF16).astype(F32)
    half = panels // 2
    dens[me] = jnp.concatenate([density[:, :half], density[:, half:]], axis=0).astype(BF16)
    lane_cluster = lax.broadcasted_iota(jnp.int32, (8, panels), 1) // block
    diagonal = jnp.concatenate(
        [jnp.where(lane_cluster == t, density, 0.0) for t in range(clusters)], axis=0
    ).astype(BF16)
    wide = dot_nt(diagonal, basis_v_wide[...])
    row_load = lax.broadcasted_iota(jnp.int32, (128, 128), 0) & 7
    lane_load = lax.broadcasted_iota(jnp.int32, (128, 128), 1) >> 4
    wide = jnp.where(row_load == lane_load, wide, 0.0)
    device = (core * (regions // 2) + plane) * members + me
    coeffs[device] = jnp.sum(wide.reshape(clusters, 8, 128), axis=1).astype(BF16)
    pl.semaphore_wait(ready, regions - 1)
    chips = regions // 2 * members

    @pl.loop(1, chips)
    def _(turn):
        step = chips - turn
        there = lax.rem(plane + step // members, regions // 2) * 2 + core
        push_to(coeffs.at[device], coeffs.at[device], coeff_sems, there, member_at(lax.rem(step, members))).start()

    push_all(dens, dens_sems)

    coeff_part = coeffs.at[pl.ds(0, chips - 1)]
    coeff_pushed = push(coeff_part, coeff_part, coeff_sems, 1)
    coeff_pushed.wait_recv()
    side = coeffs.at[pl.ds(pl.multiple_of(core * chips, chips), chips)]
    side_pushed = push_to(side, side, side_sems, region + 1 - 2 * core, me)
    side_pushed.start()
    near_load.wait()
    pushed(dens, dens_sems).wait_recv()
    left = lax.broadcasted_iota(jnp.int32, (8, 128), 1) < block

    @pl.loop(0, members)
    def _(m):
        rows = dens[m].astype(F32)
        for h in range(2):
            for g in range(half // 128):
                both = rows[h * 8 : h * 8 + 8, g * 128 : (g + 1) * 128]
                turned = pltpu.roll(both, block, axis=1)
                at = m * clusters + h * (clusters // 2) + g * 2
                table[at] = jnp.where(left, both, turned)
                table[at + 1] = jnp.where(left, turned, both)

    slots = near_cols.shape[1]
    unused = table.shape[0] - 1

    def near_pair(g):
        picked = []
        for h in range(2):
            t = 2 * g + h
            count = near_count[t]
            parts = []
            for j in range(0, slots, 2):
                first = jnp.where(j < count, near_cols[t, j], unused)
                second = jnp.where(j + 1 < count, near_cols[t, j + 1], unused)
                parts.append(jnp.where(left, table[first], table[second]))
            picked.append(jnp.concatenate(parts, axis=1))
        both = jnp.concatenate(picked, axis=0).astype(BF16)
        blocks = near[pl.ds(2 * g, 2)].reshape(2 * block, slots * block)
        result = dot_nt(both, blocks)
        near_pot[:, pl.ds(pl.multiple_of(g * 128, 128), 128)] = jnp.where(left, result[:8], result[8:])

    @pl.loop(0, clusters // 2, unroll=8)
    def _(g):
        near_pair(g)

    side_pushed.wait_recv()

    @pl.loop(0, members)
    def _(i):
        for r in range(regions):
            at = pl.multiple_of((r * members + i) * clusters, clusters)
            d = (r % 2 * (regions // 2) + r // 2) * members + i
            coeff_rows[pl.ds(at, clusters), :] = coeffs[d].astype(F32)

    own_q = lax.broadcasted_iota(jnp.int32, (256, 128), 0) & 15
    lane_q = lax.broadcasted_iota(jnp.int32, (256, 128), 1) & 15
    same_q = own_q == lane_q

    @pl.loop(0, clusters)
    def _(t):
        for a in range(32):
            picked_rows[pl.ds(t * 32 + a, 1), :] = coeff_rows[pl.ds(far_cols[t, a], 1), :]

    for t in range(clusters):
        rows = picked_rows[t * 32 : t * 32 + 32].astype(BF16)
        product = dot(coup_cat[t], jnp.concatenate([rows, rows], axis=0))
        product = jnp.where(same_q, product, 0.0)
        folded[t * 16 : t * 16 + 16] = jnp.sum(product.reshape(16, 16, 128), axis=1)

    fold = jnp.where(
        lax.broadcasted_iota(jnp.int32, (8, 128), 0)
        == lax.broadcasted_iota(jnp.int32, (8, 128), 1) >> 4,
        1.0,
        0.0,
    )
    fold = jnp.concatenate([fold, fold], axis=0).astype(BF16)
    folded_high, folded_low = split(folded[...])
    far_coef = (dot_nt(fold, folded_high) + dot_nt(fold, folded_low))[:8]
    far_high, far_low = split(far_coef)
    far_both = jnp.concatenate([far_high.astype(F32), far_low.astype(F32)], axis=0).astype(BF16)
    with_high = dot(far_both, basis_u_high[...])
    with_low = dot(far_both, basis_u_low[...])
    potential = near_pot[...] + (with_high[:8] + with_high[8:] + with_low[:8])

    scaled = -0.25 * areas[...]
    for c in range(3):
        moved[c] = potential * (scaled * normals[c : c + 1, :])

    def build_spread(at):
        @pl.loop(0, panels // 256)
        def _(i):
            base = pl.multiple_of(i * 256, 256)
            load = [moved[c, :, pl.ds(base, 256)] for c in range(3)]
            for k in range(4):
                lo = (nodes[k : k + 1, pl.ds(base, 256)] >> 7) & 7
                rows = []
                for q in range(8):
                    hit = jnp.broadcast_to(lo == q, (8, 256))
                    rows += [jnp.where(hit, load[c], 0.0) for c in range(3)]
                columns = pl.ds(k * panels + base, 256)
                spread[at, :, columns] = jnp.concatenate(rows, axis=0).astype(BF16)

    build_spread(0)

    partial = force_out.at[pl.ds(0, 12)]
    partial_pushed = push(partial, partial, force_sems, 1)

    def upper_sum(to_y):
        total = upper_own[to_y]
        for turn in range(1, 4):
            total = total + upper_in[lax.rem(x + turn, 4), to_y].astype(F32)
        return total

    def lower_sum(to_x):
        total = lower_own[to_x]
        for turn in range(1, 4):
            total = total + lower_in[lax.rem(y + turn, 4), to_x].astype(F32)
        return total

    def second_hop():
        partial_pushed.wait_recv()
        for turn in (2, 1, 3):
            last_out[turn, upper] = upper_sum(lax.rem(y + turn, 4)).astype(BF16)
            piece = (last_out.at[turn, upper], last_in.at[turn, upper])
            push_to(*piece, last_sems, region, along_y(turn)).start()
            last_out[turn, lower] = lower_sum(lax.rem(x + turn, 4)).astype(BF16)
            piece = (last_out.at[turn, lower], last_in.at[turn, lower])
            push_to(*piece, last_sems, region, along_x(turn)).start()

    @pl.loop(0, 5)
    def _(i):
        @pl.when(i == 4)
        def _():
            second_hop()
            for c in range(3):
                moved[c] = moved[c] - moved[c].astype(BF16).astype(F32)
            build_spread(1)

        columns = pl.ds(pl.multiple_of((i - i // 4) * 512, 512), 512)
        sums = dot(spread[i // 4], hot_turned[:, columns])

        @pl.when(i < 4)
        def _():
            for h in range(4):
                ahead = lax.rem(h + i + 1, 4)
                to_x, to_y = lax.rem(x + h, 4), lax.rem(y + ahead, 4)
                at = i * 4 + h
                sums_of = sums[:, h * 128 : (h + 1) * 128]
                force_out[at] = sums_of.astype(BF16)
                if h == 0:
                    upper_own[to_y] = sums_of[:half_rows]
                else:
                    push_to(
                        force_out.at[at, upper], upper_in.at[x, to_y], force_sems, region, to_x * 4 + y
                    ).start()

                @pl.when(ahead == 0)
                def _():
                    lower_own[to_x] = sums_of[half_rows:]

                @pl.when(ahead != 0)
                def _():
                    push_to(
                        force_out.at[at, lower], lower_in.at[y, to_x], force_sems, region, x * 4 + to_y
                    ).start()

        @pl.when(i == 4)
        def _():
            upper_own[y] += sums[:half_rows, :128]
            lower_own[x] += sums[half_rows:, :128]

    total = jnp.concatenate([upper_sum(y), lower_sum(x)], axis=0)
    last = last_out.at[pl.ds(1, 3)]
    last_pushed = push(last, last, last_sems, 1)
    last_pushed.wait_recv()
    for turn in range(1, 4):
        total = total + last_in[turn].astype(F32)
    for lo in range(8):
        for c in range(3):
            at = (lo * 3 + c) * 8
            out[c, :, lo * 128 : (lo + 1) * 128] = total[at : at + 8]

    first_pushed.wait_send()
    second_pushed.wait_send()
    pushed(dens, dens_sems).wait_send()
    coeff_pushed.wait_send()
    side_pushed.wait_send()
    partial_pushed.wait_send()
    last_pushed.wait_send()


def push_to(source, target, sems, region, member):
    return pltpu.make_async_remote_copy(
        src_ref=source,
        dst_ref=target,
        send_sem=sems.at[0],
        recv_sem=sems.at[1],
        device_id=(region, member),
        device_id_type=MESH,
    )


def body(
    regions,
    members,
    velocity,
    normals,
    areas,
    panel_nodes,
    near_blocks,
    near_cols,
    near_count,
    basis_v,
    basis_u,
    coupling,
    far_cols,
):
    nodes = velocity.shape[2]
    panels = normals.shape[1]
    clusters, block = near_blocks.shape[0], near_blocks.shape[1]
    rows = 24 * nodes // 128
    lanes = members * 128
    vmem = pl.BlockSpec(memory_space=pltpu.VMEM)
    hbm = pl.BlockSpec(memory_space=pl.ANY)
    dma = pltpu.SemaphoreType.DMA
    result = pl.pallas_call(
        functools.partial(kernel, regions, members),
        out_shape=pltpu.VMEM((3, 8, nodes), F32),
        in_specs=[hbm] * 11,
        out_specs=vmem,
        scratch_shapes=[
            pltpu.SMEM(near_cols.shape, jnp.int32),
            pltpu.SMEM(near_count.shape, jnp.int32),
            pltpu.SMEM(far_cols.shape, jnp.int32),
            pltpu.VMEM((3, 8, nodes), F32),
            pltpu.VMEM(normals.shape, F32),
            pltpu.VMEM((1, panels), F32),
            pltpu.VMEM((4, panels), jnp.int32),
            pltpu.VMEM((clusters, 16, block), BF16),
            pltpu.VMEM((clusters, 16, block), F32),
            pltpu.VMEM(near_blocks.shape, BF16),
            pltpu.VMEM((clusters, 16, 16, 32), F32),
            pltpu.VMEM((lanes, 4 * panels), BF16),
            pltpu.VMEM((4 * panels, lanes), BF16),
            pltpu.VMEM((panels, 8), F32),
            pltpu.VMEM((4, 4, rows, 128), BF16),
            pltpu.VMEM((rows, lanes), BF16),
            pltpu.VMEM((rows, 128), BF16),
            pltpu.VMEM((3, 8, panels), F32),
            pltpu.VMEM((members, 16, panels // 2), BF16),
            pltpu.VMEM((members * clusters + 1, 8, 128), F32),
            pltpu.VMEM((members * regions, clusters, 128), BF16),
            pltpu.VMEM((members * regions * clusters, 128), F32),
            pltpu.VMEM((clusters * 32, 128), F32),
            pltpu.VMEM((clusters, 256, 64), BF16),
            pltpu.VMEM((clusters * 16, 128), F32),
            pltpu.VMEM((128, panels), BF16),
            pltpu.VMEM((clusters * 16, panels), BF16),
            pltpu.VMEM((clusters * 16, panels), BF16),
            pltpu.VMEM((8, panels), F32),
            pltpu.VMEM((2, rows, 4 * panels), BF16),
            pltpu.VMEM((members, rows, 128), BF16),
            pltpu.VMEM((4, rows // 2, 128), F32),
            pltpu.VMEM((4, rows // 2, 128), F32),
            pltpu.VMEM((4, 4, rows // 2, 128), BF16),
            pltpu.VMEM((4, 4, rows // 2, 128), BF16),
            pltpu.VMEM((4, rows, 128), BF16),
            pltpu.VMEM((4, rows, 128), BF16),
            dma((11,)),
            dma((2,)),
            dma((2,)),
            dma((2,)),
            dma((2,)),
            dma((2,)),
            dma((2,)),
            dma((2,)),
            pltpu.SemaphoreType.REGULAR,
        ],
        compiler_params=pltpu.CompilerParams(
            collective_id=0, has_side_effects=True, vmem_limit_bytes=56 * 1024 * 1024
        ),
        name="hull",
    )(
        near_cols,
        near_count,
        far_cols,
        jnp.transpose(velocity, (1, 0, 2)),
        normals,
        areas.reshape(1, panels),
        panel_nodes.T,
        jnp.transpose(basis_v, (0, 2, 1)),
        jnp.transpose(basis_u, (0, 2, 1)),
        near_blocks,
        jnp.transpose(coupling, (0, 2, 3, 1)),
    )
    return jnp.transpose(result, (1, 0, 2))


def solution(mesh):
    both = ("region", "member")
    placed = (
        P(None, None, both),
        P(None, both),
        P(both),
        P(both, None),
        P(both, None, None),
        P(both, None),
        P(both),
        P(both, None, None),
        P(both, None, None),
        P(both, None, None, None),
        P(both, None),
    )
    return jax.shard_map(
        functools.partial(body, mesh.shape["region"], mesh.shape["member"]),
        mesh=mesh,
        in_specs=placed,
        out_specs=P(None, None, both),
        check_vma=False,
    )
```

```python
import functools

import jax
import jax.numpy as jnp
from jax import lax
from jax.experimental import pallas as pl
from jax.experimental.pallas import tpu as pltpu
from jax.sharding import PartitionSpec as P

MESH = pl.DeviceIdType.MESH
F32 = jnp.float32
BF16 = jnp.bfloat16
NT = (((1,), (1,)), ((), ()))


def split(x):
    high = x.astype(BF16)
    return high, (x - high.astype(F32)).astype(BF16)


def dot(a, b):
    return jnp.dot(a, b, preferred_element_type=F32)


def dot_nt(a, b):
    return lax.dot_general(a, b, NT, preferred_element_type=F32)


def kernel(
    regions,
    members,
    near_cols_hbm,
    near_count_hbm,
    far_cols_hbm,
    velocity_hbm,
    normals_hbm,
    areas_hbm,
    nodes_hbm,
    basis_v_hbm,
    basis_u_hbm,
    near_hbm,
    coupling_hbm,
    out,
    near_cols,
    near_count,
    far_cols,
    velocity,
    normals,
    areas,
    nodes,
    basis_v,
    basis_u,
    near,
    coupling,
    hot,
    hot_turned,
    column_of,
    motion,
    motion_cat,
    motion_low,
    moved,
    dens,
    table,
    coeffs,
    coeff_rows,
    picked_rows,
    coup_cat,
    folded,
    basis_v_wide,
    basis_u_high,
    basis_u_low,
    near_pot,
    spread,
    force_out,
    upper_own,
    lower_own,
    upper_in,
    lower_in,
    last_out,
    last_in,
    load_sems,
    motion_sems,
    relay_sems,
    dens_sems,
    coeff_sems,
    side_sems,
    force_sems,
    last_sems,
    ready,
):
    region = lax.axis_index("region")
    me = lax.axis_index("member")
    x, y = me // 4, lax.rem(me, 4)
    plane, core = region // 2, lax.rem(region, 2)
    clusters, block = near.shape[0], near.shape[1]
    panels = nodes.shape[1]
    loads = velocity.shape[1]

    def member_at(step):
        return lax.rem(me + step, members)

    def along_x(turn):
        return lax.rem(x + turn, 4) * 4 + y

    def along_y(turn):
        return x * 4 + lax.rem(y + turn, 4)

    def load(source, target, at):
        return pltpu.make_async_copy(source, target, load_sems.at[at])

    velocity_load = load(velocity_hbm, velocity, 0)
    nodes_load = load(nodes_hbm, nodes, 1)
    near_load = load(near_hbm, near, 2)
    coup_load = load(coupling_hbm, coupling, 3)
    small_loads = [
        load(normals_hbm, normals, 4),
        load(areas_hbm, areas, 5),
        load(basis_v_hbm, basis_v, 6),
        load(basis_u_hbm, basis_u, 7),
        load(near_cols_hbm, near_cols, 8),
        load(near_count_hbm, near_count, 9),
        load(far_cols_hbm, far_cols, 10),
    ]
    velocity_load.start()
    barrier = pltpu.get_barrier_semaphore()
    for turn in range(1, 4):
        for peer in (along_x(turn), along_y(turn)):
            pl.semaphore_signal(barrier, inc=1, device_id=(region, peer), device_id_type=MESH)
    for step in range(1, regions):
        pl.semaphore_signal(
            barrier, inc=1, device_id=(lax.rem(region + step, regions), me), device_id_type=MESH
        )

    nodes_load.start()
    near_load.start()
    coup_load.start()
    for copy in small_loads:
        copy.start()

    def push(source, target, sems, step):
        return push_to(source, target, sems, region, member_at(step))

    def push_all(rows, sems):
        @pl.loop(1, members)
        def _(step):
            push(rows.at[me], rows.at[me], sems, step).start()

    def pushed(rows, sems):
        part = rows.at[pl.ds(0, members - 1)]
        return push(part, part, sems, 1)

    velocity_load.wait()
    own = jnp.concatenate(
        [velocity[c, :, lo * 128 : (lo + 1) * 128] for lo in range(8) for c in range(3)], axis=0
    )
    own_high, own_low = split(own)
    motion[x, y] = own_high
    motion_low[...] = own_low
    pl.semaphore_wait(barrier, 6 + regions - 1)
    half_rows = motion.shape[2] // 2
    upper, lower = pl.ds(0, half_rows), pl.ds(half_rows, half_rows)

    for turn in (2, 1, 3):
        mine = motion.at[x, y, upper]
        push_to(mine, mine, motion_sems, region, along_x(turn)).start()
        mine = motion.at[x, y, lower]
        push_to(mine, mine, motion_sems, region, along_y(turn)).start()

    nodes_load.wait()
    node = nodes[...]
    lanes_low, owner = (node & 127).astype(F32), (node >> 10).astype(F32)
    ahead_x = ((node >> 12) - x) & 3
    ahead_y = (((node >> 10) & 3) - y) & 3
    stand = (((ahead_y - ahead_x + 3) & 3) * 4 + ahead_x).astype(F32)
    column_of[...] = jnp.transpose(jnp.concatenate([lanes_low, stand], axis=0))
    one, zero = jnp.ones((), BF16), jnp.zeros((), BF16)

    @pl.loop(0, 8)
    def _(i):
        base = pl.multiple_of(i * 16, 16)
        rows = (lax.broadcasted_iota(jnp.int32, (16, panels), 0) + base).astype(F32).astype(BF16)
        for k in range(4):
            low = jnp.broadcast_to(lanes_low[k : k + 1], (16, panels)).astype(BF16)
            holder = jnp.broadcast_to(owner[k : k + 1], (16, panels)).astype(BF16)
            found = jnp.where(low == rows, one, zero)
            for m in range(members):
                hot[pl.ds(m * 128 + base, 16), k * panels : (k + 1) * panels] = jnp.where(
                    holder == float(m), found, zero
                )

    firsts = motion.at[0, pl.ds(0, 3)]
    first_pushed = push(firsts, firsts, motion_sems, 1)
    first_pushed.wait_recv()
    for turn in (2, 1, 3):
        line = motion.at[:, y, upper]
        push_to(line, line, relay_sems, region, along_y(turn)).start()
        line = motion.at[x, :, lower]
        push_to(line, line, relay_sems, region, along_x(turn)).start()
    for step in range(1, regions):
        pl.semaphore_signal(
            ready, inc=1, device_id=(lax.rem(region + step, regions), me), device_id_type=MESH
        )
    seconds = motion.at[pl.ds(0, 3)]
    second_pushed = push(seconds, seconds, relay_sems, 1)

    @pl.loop(0, panels // 16)
    def _(i):
        base = pl.multiple_of(i * 16, 16)
        lanes = lax.broadcasted_iota(jnp.int32, (16, 128), 1).astype(F32).astype(BF16)
        for k in range(4):
            low = jnp.broadcast_to(column_of[pl.ds(base, 16), k : k + 1], (16, 128)).astype(BF16)
            holder = jnp.broadcast_to(column_of[pl.ds(base, 16), k + 4 : k + 5], (16, 128)).astype(BF16)
            found = jnp.where(low == lanes, one, zero)
            for m in range(members):
                hot_turned[pl.ds(k * panels + base, 16), m * 128 : (m + 1) * 128] = jnp.where(
                    holder == float(m), found, zero
                )

    for copy in small_loads:
        copy.wait()
    for g in range(clusters // 2):
        pair = jnp.concatenate([basis_v[2 * g], basis_v[2 * g + 1]], axis=1)
        basis_v_wide[:, g * 128 : (g + 1) * 128] = jnp.concatenate([pair] * loads, axis=0)
    basis_u_high[...] = jnp.zeros_like(basis_u_high)
    basis_u_low[...] = jnp.zeros_like(basis_u_low)
    empty = jnp.zeros((16, block), F32)
    for t in range(clusters):
        parts = [basis_u[t], empty] if t % 2 == 0 else [empty, basis_u[t]]
        high, low = split(jnp.concatenate(parts, axis=1))
        where = (slice(t * 16, t * 16 + 16), slice(t // 2 * 128, t // 2 * 128 + 128))
        basis_u_high[where] = high
        basis_u_low[where] = low
    coup_load.wait()

    @pl.loop(0, clusters)
    def _(t):
        high, low = split(coupling[t].reshape(256, 32))
        coup_cat[t] = jnp.concatenate([high, low], axis=1)

    table[table.shape[0] - 1] = jnp.zeros((8, 128), F32)

    second_pushed.wait_recv()
    for m in range(members):
        motion_cat[:, m * 128 : (m + 1) * 128] = motion[m // 4, m % 4]
    own_rows = pl.ds(pl.multiple_of(me * 128, 128), 128)

    for c in range(3):
        moved[c] = jnp.zeros((8, panels), F32)

    @pl.loop(0, 4)
    def _(k):
        columns = pl.ds(pl.multiple_of(k * panels, panels), panels)
        rows = dot(motion_cat[...], hot[:, columns]) + dot(motion_low[...], hot[own_rows, columns])
        lo = (nodes[pl.ds(k, 1), :] >> 7) & 7
        for c in range(3):
            total = moved[c]
            for q in range(8):
                at = (q * 3 + c) * 8
                total = total + jnp.where(jnp.broadcast_to(lo == q, (8, panels)), rows[at : at + 8], 0.0)
            moved[c] = total

    normal_vel = 0.25 * (
        moved[0] * normals[0:1, :] + moved[1] * normals[1:2, :] + moved[2] * normals[2:3, :]
    )
    density = normal_vel.astype(BF16).astype(F32)
    half = panels // 2
    dens[me] = jnp.concatenate([density[:, :half], density[:, half:]], axis=0).astype(BF16)
    lane_cluster = lax.broadcasted_iota(jnp.int32, (8, panels), 1) // block
    diagonal = jnp.concatenate(
        [jnp.where(lane_cluster == t, density, 0.0) for t in range(clusters)], axis=0
    ).astype(BF16)
    wide = dot_nt(diagonal, basis_v_wide[...])
    row_load = lax.broadcasted_iota(jnp.int32, (128, 128), 0) & 7
    lane_load = lax.broadcasted_iota(jnp.int32, (128, 128), 1) >> 4
    wide = jnp.where(row_load == lane_load, wide, 0.0)
    device = (core * (regions // 2) + plane) * members + me
    coeffs[device] = jnp.sum(wide.reshape(clusters, 8, 128), axis=1).astype(BF16)
    pl.semaphore_wait(ready, regions - 1)
    chips = regions // 2 * members

    @pl.loop(1, chips, unroll=7)
    def _(turn):
        step = chips - turn
        there = lax.rem(plane + step // members, regions // 2) * 2 + core
        push_to(coeffs.at[device], coeffs.at[device], coeff_sems, there, member_at(lax.rem(step, members))).start()

    push_all(dens, dens_sems)

    coeff_part = coeffs.at[pl.ds(0, chips - 1)]
    coeff_pushed = push(coeff_part, coeff_part, coeff_sems, 1)
    coeff_pushed.wait_recv()
    side = coeffs.at[pl.ds(pl.multiple_of(core * chips, chips), chips)]
    side_pushed = push_to(side, side, side_sems, region + 1 - 2 * core, me)
    side_pushed.start()
    near_load.wait()
    pushed(dens, dens_sems).wait_recv()
    left = lax.broadcasted_iota(jnp.int32, (8, 128), 1) < block

    @pl.loop(0, members, unroll=16)
    def _(m):
        rows = dens[m].astype(F32)
        for h in range(2):
            for g in range(half // 128):
                both = rows[h * 8 : h * 8 + 8, g * 128 : (g + 1) * 128]
                turned = pltpu.roll(both, block, axis=1)
                at = m * clusters + h * (clusters // 2) + g * 2
                table[at] = jnp.where(left, both, turned)
                table[at + 1] = jnp.where(left, turned, both)

    slots = near_cols.shape[1]
    unused = table.shape[0] - 1

    def near_pair(g):
        picked = []
        for h in range(2):
            t = 2 * g + h
            count = near_count[t]
            parts = []
            for j in range(0, slots, 2):
                first = jnp.where(j < count, near_cols[t, j], unused)
                second = jnp.where(j + 1 < count, near_cols[t, j + 1], unused)
                parts.append(jnp.where(left, table[first], table[second]))
            picked.append(jnp.concatenate(parts, axis=1))
        both = jnp.concatenate(picked, axis=0).astype(BF16)
        blocks = near[pl.ds(2 * g, 2)].reshape(2 * block, slots * block)
        result = dot_nt(both, blocks)
        near_pot[:, pl.ds(pl.multiple_of(g * 128, 128), 128)] = jnp.where(left, result[:8], result[8:])

    @pl.loop(0, clusters // 2, unroll=8)
    def _(g):
        near_pair(g)

    side_pushed.wait_recv()

    @pl.loop(0, members, unroll=2)
    def _(i):
        for r in range(regions):
            at = pl.multiple_of((r * members + i) * clusters, clusters)
            d = (r % 2 * (regions // 2) + r // 2) * members + i
            coeff_rows[pl.ds(at, clusters), :] = coeffs[d].astype(F32)

    own_q = lax.broadcasted_iota(jnp.int32, (256, 128), 0) & 15
    lane_q = lax.broadcasted_iota(jnp.int32, (256, 128), 1) & 15
    same_q = own_q == lane_q

    @pl.loop(0, clusters, unroll=2)
    def _(t):
        for a in range(32):
            picked_rows[pl.ds(t * 32 + a, 1), :] = coeff_rows[pl.ds(far_cols[t, a], 1), :]

    for t in range(clusters):
        rows = picked_rows[t * 32 : t * 32 + 32].astype(BF16)
        product = dot(coup_cat[t], jnp.concatenate([rows, rows], axis=0))
        product = jnp.where(same_q, product, 0.0)
        folded[t * 16 : t * 16 + 16] = jnp.sum(product.reshape(16, 16, 128), axis=1)

    fold = jnp.where(
        lax.broadcasted_iota(jnp.int32, (8, 128), 0)
        == lax.broadcasted_iota(jnp.int32, (8, 128), 1) >> 4,
        1.0,
        0.0,
    )
    fold = jnp.concatenate([fold, fold], axis=0).astype(BF16)
    folded_high, folded_low = split(folded[...])
    far_coef = (dot_nt(fold, folded_high) + dot_nt(fold, folded_low))[:8]
    far_high, far_low = split(far_coef)
    far_both = jnp.concatenate([far_high.astype(F32), far_low.astype(F32)], axis=0).astype(BF16)
    with_high = dot(far_both, basis_u_high[...])
    with_low = dot(far_both, basis_u_low[...])
    potential = near_pot[...] + (with_high[:8] + with_high[8:] + with_low[:8])

    scaled = -0.25 * areas[...]
    for c in range(3):
        moved[c] = potential * (scaled * normals[c : c + 1, :])

    def build_spread(at):
        @pl.loop(0, panels // 256)
        def _(i):
            base = pl.multiple_of(i * 256, 256)
            load = [moved[c, :, pl.ds(base, 256)] for c in range(3)]
            for k in range(4):
                lo = (nodes[k : k + 1, pl.ds(base, 256)] >> 7) & 7
                rows = []
                for q in range(8):
                    hit = jnp.broadcast_to(lo == q, (8, 256))
                    rows += [jnp.where(hit, load[c], 0.0) for c in range(3)]
                columns = pl.ds(k * panels + base, 256)
                spread[at, :, columns] = jnp.concatenate(rows, axis=0).astype(BF16)

    build_spread(0)

    partial = force_out.at[pl.ds(0, 12)]
    partial_pushed = push(partial, partial, force_sems, 1)

    def upper_sum(to_y):
        total = upper_own[to_y]
        for turn in range(1, 4):
            total = total + upper_in[lax.rem(x + turn, 4), to_y].astype(F32)
        return total

    def lower_sum(to_x):
        total = lower_own[to_x]
        for turn in range(1, 4):
            total = total + lower_in[lax.rem(y + turn, 4), to_x].astype(F32)
        return total

    def second_hop():
        partial_pushed.wait_recv()
        for turn in (2, 1, 3):
            last_out[turn, upper] = upper_sum(lax.rem(y + turn, 4)).astype(BF16)
            piece = (last_out.at[turn, upper], last_in.at[turn, upper])
            push_to(*piece, last_sems, region, along_y(turn)).start()
            last_out[turn, lower] = lower_sum(lax.rem(x + turn, 4)).astype(BF16)
            piece = (last_out.at[turn, lower], last_in.at[turn, lower])
            push_to(*piece, last_sems, region, along_x(turn)).start()

    @pl.loop(0, 5)
    def _(i):
        @pl.when(i == 4)
        def _():
            second_hop()
            for c in range(3):
                moved[c] = moved[c] - moved[c].astype(BF16).astype(F32)
            build_spread(1)

        columns = pl.ds(pl.multiple_of((i - i // 4) * 512, 512), 512)
        sums = dot(spread[i // 4], hot_turned[:, columns])

        @pl.when(i < 4)
        def _():
            for h in range(4):
                ahead = lax.rem(h + i + 1, 4)
                to_x, to_y = lax.rem(x + h, 4), lax.rem(y + ahead, 4)
                at = i * 4 + h
                sums_of = sums[:, h * 128 : (h + 1) * 128]
                force_out[at] = sums_of.astype(BF16)
                if h == 0:
                    upper_own[to_y] = sums_of[:half_rows]
                else:
                    push_to(
                        force_out.at[at, upper], upper_in.at[x, to_y], force_sems, region, to_x * 4 + y
                    ).start()

                @pl.when(ahead == 0)
                def _():
                    lower_own[to_x] = sums_of[half_rows:]

                @pl.when(ahead != 0)
                def _():
                    push_to(
                        force_out.at[at, lower], lower_in.at[y, to_x], force_sems, region, x * 4 + to_y
                    ).start()

        @pl.when(i == 4)
        def _():
            upper_own[y] += sums[:half_rows, :128]
            lower_own[x] += sums[half_rows:, :128]

    total = jnp.concatenate([upper_sum(y), lower_sum(x)], axis=0)
    last = last_out.at[pl.ds(1, 3)]
    last_pushed = push(last, last, last_sems, 1)
    last_pushed.wait_recv()
    for turn in range(1, 4):
        total = total + last_in[turn].astype(F32)
    for lo in range(8):
        for c in range(3):
            at = (lo * 3 + c) * 8
            out[c, :, lo * 128 : (lo + 1) * 128] = total[at : at + 8]

    first_pushed.wait_send()
    second_pushed.wait_send()
    pushed(dens, dens_sems).wait_send()
    coeff_pushed.wait_send()
    side_pushed.wait_send()
    partial_pushed.wait_send()
    last_pushed.wait_send()


def push_to(source, target, sems, region, member):
    return pltpu.make_async_remote_copy(
        src_ref=source,
        dst_ref=target,
        send_sem=sems.at[0],
        recv_sem=sems.at[1],
        device_id=(region, member),
        device_id_type=MESH,
    )


def body(
    regions,
    members,
    velocity,
    normals,
    areas,
    panel_nodes,
    near_blocks,
    near_cols,
    near_count,
    basis_v,
    basis_u,
    coupling,
    far_cols,
):
    nodes = velocity.shape[2]
    panels = normals.shape[1]
    clusters, block = near_blocks.shape[0], near_blocks.shape[1]
    rows = 24 * nodes // 128
    lanes = members * 128
    vmem = pl.BlockSpec(memory_space=pltpu.VMEM)
    hbm = pl.BlockSpec(memory_space=pl.ANY)
    dma = pltpu.SemaphoreType.DMA
    result = pl.pallas_call(
        functools.partial(kernel, regions, members),
        out_shape=pltpu.VMEM((3, 8, nodes), F32),
        in_specs=[hbm] * 11,
        out_specs=vmem,
        scratch_shapes=[
            pltpu.SMEM(near_cols.shape, jnp.int32),
            pltpu.SMEM(near_count.shape, jnp.int32),
            pltpu.SMEM(far_cols.shape, jnp.int32),
            pltpu.VMEM((3, 8, nodes), F32),
            pltpu.VMEM(normals.shape, F32),
            pltpu.VMEM((1, panels), F32),
            pltpu.VMEM((4, panels), jnp.int32),
            pltpu.VMEM((clusters, 16, block), BF16),
            pltpu.VMEM((clusters, 16, block), F32),
            pltpu.VMEM(near_blocks.shape, BF16),
            pltpu.VMEM((clusters, 16, 16, 32), F32),
            pltpu.VMEM((lanes, 4 * panels), BF16),
            pltpu.VMEM((4 * panels, lanes), BF16),
            pltpu.VMEM((panels, 8), F32),
            pltpu.VMEM((4, 4, rows, 128), BF16),
            pltpu.VMEM((rows, lanes), BF16),
            pltpu.VMEM((rows, 128), BF16),
            pltpu.VMEM((3, 8, panels), F32),
            pltpu.VMEM((members, 16, panels // 2), BF16),
            pltpu.VMEM((members * clusters + 1, 8, 128), F32),
            pltpu.VMEM((members * regions, clusters, 128), BF16),
            pltpu.VMEM((members * regions * clusters, 128), F32),
            pltpu.VMEM((clusters * 32, 128), F32),
            pltpu.VMEM((clusters, 256, 64), BF16),
            pltpu.VMEM((clusters * 16, 128), F32),
            pltpu.VMEM((128, panels), BF16),
            pltpu.VMEM((clusters * 16, panels), BF16),
            pltpu.VMEM((clusters * 16, panels), BF16),
            pltpu.VMEM((8, panels), F32),
            pltpu.VMEM((2, rows, 4 * panels), BF16),
            pltpu.VMEM((members, rows, 128), BF16),
            pltpu.VMEM((4, rows // 2, 128), F32),
            pltpu.VMEM((4, rows // 2, 128), F32),
            pltpu.VMEM((4, 4, rows // 2, 128), BF16),
            pltpu.VMEM((4, 4, rows // 2, 128), BF16),
            pltpu.VMEM((4, rows, 128), BF16),
            pltpu.VMEM((4, rows, 128), BF16),
            dma((11,)),
            dma((2,)),
            dma((2,)),
            dma((2,)),
            dma((2,)),
            dma((2,)),
            dma((2,)),
            dma((2,)),
            pltpu.SemaphoreType.REGULAR,
        ],
        compiler_params=pltpu.CompilerParams(
            collective_id=0, has_side_effects=True, vmem_limit_bytes=56 * 1024 * 1024
        ),
        name="hull",
    )(
        near_cols,
        near_count,
        far_cols,
        jnp.transpose(velocity, (1, 0, 2)),
        normals,
        areas.reshape(1, panels),
        panel_nodes.T,
        jnp.transpose(basis_v, (0, 2, 1)),
        jnp.transpose(basis_u, (0, 2, 1)),
        near_blocks,
        jnp.transpose(coupling, (0, 2, 3, 1)),
    )
    return jnp.transpose(result, (1, 0, 2))


def solution(mesh):
    both = ("region", "member")
    placed = (
        P(None, None, both),
        P(None, both),
        P(both),
        P(both, None),
        P(both, None, None),
        P(both, None),
        P(both),
        P(both, None, None),
        P(both, None, None),
        P(both, None, None, None),
        P(both, None),
    )
    return jax.shard_map(
        functools.partial(body, mesh.shape["region"], mesh.shape["member"]),
        mesh=mesh,
        in_specs=placed,
        out_specs=P(None, None, both),
        check_vma=False,
    )
```

```python
import functools

import jax
import jax.numpy as jnp
from jax import lax
from jax.experimental import pallas as pl
from jax.experimental.pallas import tpu as pltpu
from jax.sharding import PartitionSpec as P

MESH = pl.DeviceIdType.MESH
F32 = jnp.float32
BF16 = jnp.bfloat16
NT = (((1,), (1,)), ((), ()))


def split(x):
    high = x.astype(BF16)
    return high, (x - high.astype(F32)).astype(BF16)


def dot(a, b):
    return jnp.dot(a, b, preferred_element_type=F32)


def dot_nt(a, b):
    return lax.dot_general(a, b, NT, preferred_element_type=F32)


def kernel(
    regions,
    members,
    near_cols_hbm,
    near_count_hbm,
    far_cols_hbm,
    velocity_hbm,
    normals_hbm,
    areas_hbm,
    nodes_hbm,
    basis_v_hbm,
    basis_u_hbm,
    near_hbm,
    coupling_hbm,
    out,
    near_cols,
    near_count,
    far_cols,
    velocity,
    normals,
    areas,
    nodes,
    basis_v,
    basis_u,
    near,
    coupling,
    hot,
    hot_turned,
    column_of,
    motion,
    motion_cat,
    motion_low,
    moved,
    dens,
    table,
    coeffs,
    coeff_rows,
    picked_rows,
    coup_cat,
    folded,
    basis_v_wide,
    basis_u_high,
    basis_u_low,
    near_pot,
    spread,
    force_out,
    upper_own,
    lower_own,
    upper_in,
    lower_in,
    last_out,
    last_in,
    load_sems,
    motion_sems,
    relay_sems,
    dens_sems,
    coeff_sems,
    side_sems,
    force_sems,
    last_sems,
    ready,
):
    region = lax.axis_index("region")
    me = lax.axis_index("member")
    x, y = me // 4, lax.rem(me, 4)
    plane, core = region // 2, lax.rem(region, 2)
    clusters, block = near.shape[0], near.shape[1]
    panels = nodes.shape[1]
    loads = velocity.shape[1]

    def member_at(step):
        return lax.rem(me + step, members)

    def along_x(turn):
        return lax.rem(x + turn, 4) * 4 + y

    def along_y(turn):
        return x * 4 + lax.rem(y + turn, 4)

    def load(source, target, at):
        return pltpu.make_async_copy(source, target, load_sems.at[at])

    velocity_load = load(velocity_hbm, velocity, 0)
    nodes_load = load(nodes_hbm, nodes, 1)
    near_load = load(near_hbm, near, 2)
    coup_load = load(coupling_hbm, coupling, 3)
    small_loads = [
        load(normals_hbm, normals, 4),
        load(areas_hbm, areas, 5),
        load(basis_v_hbm, basis_v, 6),
        load(basis_u_hbm, basis_u, 7),
        load(near_cols_hbm, near_cols, 8),
        load(near_count_hbm, near_count, 9),
        load(far_cols_hbm, far_cols, 10),
    ]
    velocity_load.start()
    barrier = pltpu.get_barrier_semaphore()
    for turn in range(1, 4):
        for peer in (along_x(turn), along_y(turn)):
            pl.semaphore_signal(barrier, inc=1, device_id=(region, peer), device_id_type=MESH)
    for step in range(1, regions):
        pl.semaphore_signal(
            barrier, inc=1, device_id=(lax.rem(region + step, regions), me), device_id_type=MESH
        )

    nodes_load.start()
    near_load.start()
    coup_load.start()
    for copy in small_loads:
        copy.start()

    def push(source, target, sems, step):
        return push_to(source, target, sems, region, member_at(step))

    def push_all(rows, sems):
        @pl.loop(1, members)
        def _(step):
            push(rows.at[me], rows.at[me], sems, step).start()

    def pushed(rows, sems):
        part = rows.at[pl.ds(0, members - 1)]
        return push(part, part, sems, 1)

    velocity_load.wait()
    own = jnp.concatenate(
        [velocity[c, :, lo * 128 : (lo + 1) * 128] for lo in range(8) for c in range(3)], axis=0
    )
    own_high, own_low = split(own)
    motion[x, y] = own_high
    motion_low[...] = own_low
    pl.semaphore_wait(barrier, 6 + regions - 1)
    half_rows = motion.shape[2] // 2
    upper, lower = pl.ds(0, half_rows), pl.ds(half_rows, half_rows)

    for turn in (2, 1, 3):
        mine = motion.at[x, y, upper]
        push_to(mine, mine, motion_sems, region, along_x(turn)).start()
        mine = motion.at[x, y, lower]
        push_to(mine, mine, motion_sems, region, along_y(turn)).start()

    nodes_load.wait()
    node = nodes[...]
    lanes_low, owner = (node & 127).astype(F32), (node >> 10).astype(F32)
    ahead_x = ((node >> 12) - x) & 3
    ahead_y = (((node >> 10) & 3) - y) & 3
    stand = (((ahead_y - ahead_x + 3) & 3) * 4 + ahead_x).astype(F32)
    column_of[...] = jnp.transpose(jnp.concatenate([lanes_low, stand], axis=0))
    one, zero = jnp.ones((), BF16), jnp.zeros((), BF16)

    @pl.loop(0, 8)
    def _(i):
        base = pl.multiple_of(i * 16, 16)
        rows = (lax.broadcasted_iota(jnp.int32, (16, panels), 0) + base).astype(F32).astype(BF16)
        for k in range(4):
            low = jnp.broadcast_to(lanes_low[k : k + 1], (16, panels)).astype(BF16)
            holder = jnp.broadcast_to(owner[k : k + 1], (16, panels)).astype(BF16)
            found = jnp.where(low == rows, one, zero)
            for m in range(members):
                hot[pl.ds(m * 128 + base, 16), k * panels : (k + 1) * panels] = jnp.where(
                    holder == float(m), found, zero
                )

    firsts = motion.at[0, pl.ds(0, 3)]
    first_pushed = push(firsts, firsts, motion_sems, 1)
    first_pushed.wait_recv()
    for turn in (2, 1, 3):
        line = motion.at[:, y, upper]
        push_to(line, line, relay_sems, region, along_y(turn)).start()
        line = motion.at[x, :, lower]
        push_to(line, line, relay_sems, region, along_x(turn)).start()
    for step in range(1, regions):
        pl.semaphore_signal(
            ready, inc=1, device_id=(lax.rem(region + step, regions), me), device_id_type=MESH
        )
    seconds = motion.at[pl.ds(0, 3)]
    second_pushed = push(seconds, seconds, relay_sems, 1)

    @pl.loop(0, panels // 16)
    def _(i):
        base = pl.multiple_of(i * 16, 16)
        lanes = lax.broadcasted_iota(jnp.int32, (16, 128), 1).astype(F32).astype(BF16)
        for k in range(4):
            low = jnp.broadcast_to(column_of[pl.ds(base, 16), k : k + 1], (16, 128)).astype(BF16)
            holder = jnp.broadcast_to(column_of[pl.ds(base, 16), k + 4 : k + 5], (16, 128)).astype(BF16)
            found = jnp.where(low == lanes, one, zero)
            for m in range(members):
                hot_turned[pl.ds(k * panels + base, 16), m * 128 : (m + 1) * 128] = jnp.where(
                    holder == float(m), found, zero
                )

    for copy in small_loads:
        copy.wait()
    for g in range(clusters // 2):
        pair = jnp.concatenate([basis_v[2 * g], basis_v[2 * g + 1]], axis=1)
        basis_v_wide[:, g * 128 : (g + 1) * 128] = jnp.concatenate([pair] * loads, axis=0)
    basis_u_high[...] = jnp.zeros_like(basis_u_high)
    basis_u_low[...] = jnp.zeros_like(basis_u_low)
    empty = jnp.zeros((16, block), F32)
    for t in range(clusters):
        parts = [basis_u[t], empty] if t % 2 == 0 else [empty, basis_u[t]]
        high, low = split(jnp.concatenate(parts, axis=1))
        where = (slice(t * 16, t * 16 + 16), slice(t // 2 * 128, t // 2 * 128 + 128))
        basis_u_high[where] = high
        basis_u_low[where] = low
    coup_load.wait()

    @pl.loop(0, clusters)
    def _(t):
        high, low = split(coupling[t].reshape(256, 32))
        coup_cat[t] = jnp.concatenate([high, low], axis=1)

    table[table.shape[0] - 1] = jnp.zeros((8, 128), F32)

    second_pushed.wait_recv()
    for m in range(members):
        motion_cat[:, m * 128 : (m + 1) * 128] = motion[m // 4, m % 4]
    own_rows = pl.ds(pl.multiple_of(me * 128, 128), 128)

    for c in range(3):
        moved[c] = jnp.zeros((8, panels), F32)

    @pl.loop(0, 4, unroll=2)
    def _(k):
        columns = pl.ds(pl.multiple_of(k * panels, panels), panels)
        rows = dot(motion_cat[...], hot[:, columns]) + dot(motion_low[...], hot[own_rows, columns])
        lo = (nodes[pl.ds(k, 1), :] >> 7) & 7
        for c in range(3):
            total = moved[c]
            for q in range(8):
                at = (q * 3 + c) * 8
                total = total + jnp.where(jnp.broadcast_to(lo == q, (8, panels)), rows[at : at + 8], 0.0)
            moved[c] = total

    normal_vel = 0.25 * (
        moved[0] * normals[0:1, :] + moved[1] * normals[1:2, :] + moved[2] * normals[2:3, :]
    )
    density = normal_vel.astype(BF16).astype(F32)
    half = panels // 2
    dens[me] = jnp.concatenate([density[:, :half], density[:, half:]], axis=0).astype(BF16)
    lane_cluster = lax.broadcasted_iota(jnp.int32, (8, panels), 1) // block
    diagonal = jnp.concatenate(
        [jnp.where(lane_cluster == t, density, 0.0) for t in range(clusters)], axis=0
    ).astype(BF16)
    wide = dot_nt(diagonal, basis_v_wide[...])
    row_load = lax.broadcasted_iota(jnp.int32, (128, 128), 0) & 7
    lane_load = lax.broadcasted_iota(jnp.int32, (128, 128), 1) >> 4
    wide = jnp.where(row_load == lane_load, wide, 0.0)
    device = (core * (regions // 2) + plane) * members + me
    coeffs[device] = jnp.sum(wide.reshape(clusters, 8, 128), axis=1).astype(BF16)
    pl.semaphore_wait(ready, regions - 1)
    chips = regions // 2 * members

    @pl.loop(1, chips, unroll=7)
    def _(turn):
        step = chips - turn
        there = lax.rem(plane + step // members, regions // 2) * 2 + core
        push_to(coeffs.at[device], coeffs.at[device], coeff_sems, there, member_at(lax.rem(step, members))).start()

    push_all(dens, dens_sems)

    coeff_part = coeffs.at[pl.ds(0, chips - 1)]
    coeff_pushed = push(coeff_part, coeff_part, coeff_sems, 1)
    coeff_pushed.wait_recv()
    side = coeffs.at[pl.ds(pl.multiple_of(core * chips, chips), chips)]
    side_pushed = push_to(side, side, side_sems, region + 1 - 2 * core, me)
    side_pushed.start()
    near_load.wait()
    pushed(dens, dens_sems).wait_recv()
    left = lax.broadcasted_iota(jnp.int32, (8, 128), 1) < block

    @pl.loop(0, members, unroll=16)
    def _(m):
        rows = dens[m].astype(F32)
        for h in range(2):
            for g in range(half // 128):
                both = rows[h * 8 : h * 8 + 8, g * 128 : (g + 1) * 128]
                turned = pltpu.roll(both, block, axis=1)
                at = m * clusters + h * (clusters // 2) + g * 2
                table[at] = jnp.where(left, both, turned)
                table[at + 1] = jnp.where(left, turned, both)

    slots = near_cols.shape[1]
    unused = table.shape[0] - 1

    def near_pair(g):
        picked = []
        for h in range(2):
            t = 2 * g + h
            count = near_count[t]
            parts = []
            for j in range(0, slots, 2):
                first = jnp.where(j < count, near_cols[t, j], unused)
                second = jnp.where(j + 1 < count, near_cols[t, j + 1], unused)
                parts.append(jnp.where(left, table[first], table[second]))
            picked.append(jnp.concatenate(parts, axis=1))
        both = jnp.concatenate(picked, axis=0).astype(BF16)
        blocks = near[pl.ds(2 * g, 2)].reshape(2 * block, slots * block)
        result = dot_nt(both, blocks)
        near_pot[:, pl.ds(pl.multiple_of(g * 128, 128), 128)] = jnp.where(left, result[:8], result[8:])

    @pl.loop(0, clusters // 2, unroll=8)
    def _(g):
        near_pair(g)

    side_pushed.wait_recv()

    @pl.loop(0, members, unroll=2)
    def _(i):
        for r in range(regions):
            at = pl.multiple_of((r * members + i) * clusters, clusters)
            d = (r % 2 * (regions // 2) + r // 2) * members + i
            coeff_rows[pl.ds(at, clusters), :] = coeffs[d].astype(F32)

    own_q = lax.broadcasted_iota(jnp.int32, (256, 128), 0) & 15
    lane_q = lax.broadcasted_iota(jnp.int32, (256, 128), 1) & 15
    same_q = own_q == lane_q

    @pl.loop(0, clusters, unroll=2)
    def _(t):
        for a in range(32):
            picked_rows[pl.ds(t * 32 + a, 1), :] = coeff_rows[pl.ds(far_cols[t, a], 1), :]

    for t in range(clusters):
        rows = picked_rows[t * 32 : t * 32 + 32].astype(BF16)
        product = dot(coup_cat[t], jnp.concatenate([rows, rows], axis=0))
        product = jnp.where(same_q, product, 0.0)
        folded[t * 16 : t * 16 + 16] = jnp.sum(product.reshape(16, 16, 128), axis=1)

    fold = jnp.where(
        lax.broadcasted_iota(jnp.int32, (8, 128), 0)
        == lax.broadcasted_iota(jnp.int32, (8, 128), 1) >> 4,
        1.0,
        0.0,
    )
    fold = jnp.concatenate([fold, fold], axis=0).astype(BF16)
    folded_high, folded_low = split(folded[...])
    far_coef = (dot_nt(fold, folded_high) + dot_nt(fold, folded_low))[:8]
    far_high, far_low = split(far_coef)
    far_both = jnp.concatenate([far_high.astype(F32), far_low.astype(F32)], axis=0).astype(BF16)
    with_high = dot(far_both, basis_u_high[...])
    with_low = dot(far_both, basis_u_low[...])
    potential = near_pot[...] + (with_high[:8] + with_high[8:] + with_low[:8])

    scaled = -0.25 * areas[...]
    for c in range(3):
        moved[c] = potential * (scaled * normals[c : c + 1, :])

    def build_spread(at):
        @pl.loop(0, panels // 256)
        def _(i):
            base = pl.multiple_of(i * 256, 256)
            load = [moved[c, :, pl.ds(base, 256)] for c in range(3)]
            for k in range(4):
                lo = (nodes[k : k + 1, pl.ds(base, 256)] >> 7) & 7
                rows = []
                for q in range(8):
                    hit = jnp.broadcast_to(lo == q, (8, 256))
                    rows += [jnp.where(hit, load[c], 0.0) for c in range(3)]
                columns = pl.ds(k * panels + base, 256)
                spread[at, :, columns] = jnp.concatenate(rows, axis=0).astype(BF16)

    build_spread(0)

    partial = force_out.at[pl.ds(0, 12)]
    partial_pushed = push(partial, partial, force_sems, 1)

    def upper_sum(to_y):
        total = upper_own[to_y]
        for turn in range(1, 4):
            total = total + upper_in[lax.rem(x + turn, 4), to_y].astype(F32)
        return total

    def lower_sum(to_x):
        total = lower_own[to_x]
        for turn in range(1, 4):
            total = total + lower_in[lax.rem(y + turn, 4), to_x].astype(F32)
        return total

    def second_hop():
        partial_pushed.wait_recv()
        for turn in (2, 1, 3):
            last_out[turn, upper] = upper_sum(lax.rem(y + turn, 4)).astype(BF16)
            piece = (last_out.at[turn, upper], last_in.at[turn, upper])
            push_to(*piece, last_sems, region, along_y(turn)).start()
            last_out[turn, lower] = lower_sum(lax.rem(x + turn, 4)).astype(BF16)
            piece = (last_out.at[turn, lower], last_in.at[turn, lower])
            push_to(*piece, last_sems, region, along_x(turn)).start()

    @pl.loop(0, 5)
    def _(i):
        @pl.when(i == 4)
        def _():
            second_hop()
            for c in range(3):
                moved[c] = moved[c] - moved[c].astype(BF16).astype(F32)
            build_spread(1)

        columns = pl.ds(pl.multiple_of((i - i // 4) * 512, 512), 512)
        sums = dot(spread[i // 4], hot_turned[:, columns])

        @pl.when(i < 4)
        def _():
            for h in range(4):
                ahead = lax.rem(h + i + 1, 4)
                to_x, to_y = lax.rem(x + h, 4), lax.rem(y + ahead, 4)
                at = i * 4 + h
                sums_of = sums[:, h * 128 : (h + 1) * 128]
                force_out[at] = sums_of.astype(BF16)
                if h == 0:
                    upper_own[to_y] = sums_of[:half_rows]
                else:
                    push_to(
                        force_out.at[at, upper], upper_in.at[x, to_y], force_sems, region, to_x * 4 + y
                    ).start()

                @pl.when(ahead == 0)
                def _():
                    lower_own[to_x] = sums_of[half_rows:]

                @pl.when(ahead != 0)
                def _():
                    push_to(
                        force_out.at[at, lower], lower_in.at[y, to_x], force_sems, region, x * 4 + to_y
                    ).start()

        @pl.when(i == 4)
        def _():
            upper_own[y] += sums[:half_rows, :128]
            lower_own[x] += sums[half_rows:, :128]

    total = jnp.concatenate([upper_sum(y), lower_sum(x)], axis=0)
    last = last_out.at[pl.ds(1, 3)]
    last_pushed = push(last, last, last_sems, 1)
    last_pushed.wait_recv()
    for turn in range(1, 4):
        total = total + last_in[turn].astype(F32)
    for lo in range(8):
        for c in range(3):
            at = (lo * 3 + c) * 8
            out[c, :, lo * 128 : (lo + 1) * 128] = total[at : at + 8]

    first_pushed.wait_send()
    second_pushed.wait_send()
    pushed(dens, dens_sems).wait_send()
    coeff_pushed.wait_send()
    side_pushed.wait_send()
    partial_pushed.wait_send()
    last_pushed.wait_send()


def push_to(source, target, sems, region, member):
    return pltpu.make_async_remote_copy(
        src_ref=source,
        dst_ref=target,
        send_sem=sems.at[0],
        recv_sem=sems.at[1],
        device_id=(region, member),
        device_id_type=MESH,
    )


def body(
    regions,
    members,
    velocity,
    normals,
    areas,
    panel_nodes,
    near_blocks,
    near_cols,
    near_count,
    basis_v,
    basis_u,
    coupling,
    far_cols,
):
    nodes = velocity.shape[2]
    panels = normals.shape[1]
    clusters, block = near_blocks.shape[0], near_blocks.shape[1]
    rows = 24 * nodes // 128
    lanes = members * 128
    vmem = pl.BlockSpec(memory_space=pltpu.VMEM)
    hbm = pl.BlockSpec(memory_space=pl.ANY)
    dma = pltpu.SemaphoreType.DMA
    result = pl.pallas_call(
        functools.partial(kernel, regions, members),
        out_shape=pltpu.VMEM((3, 8, nodes), F32),
        in_specs=[hbm] * 11,
        out_specs=vmem,
        scratch_shapes=[
            pltpu.SMEM(near_cols.shape, jnp.int32),
            pltpu.SMEM(near_count.shape, jnp.int32),
            pltpu.SMEM(far_cols.shape, jnp.int32),
            pltpu.VMEM((3, 8, nodes), F32),
            pltpu.VMEM(normals.shape, F32),
            pltpu.VMEM((1, panels), F32),
            pltpu.VMEM((4, panels), jnp.int32),
            pltpu.VMEM((clusters, 16, block), BF16),
            pltpu.VMEM((clusters, 16, block), F32),
            pltpu.VMEM(near_blocks.shape, BF16),
            pltpu.VMEM((clusters, 16, 16, 32), F32),
            pltpu.VMEM((lanes, 4 * panels), BF16),
            pltpu.VMEM((4 * panels, lanes), BF16),
            pltpu.VMEM((panels, 8), F32),
            pltpu.VMEM((4, 4, rows, 128), BF16),
            pltpu.VMEM((rows, lanes), BF16),
            pltpu.VMEM((rows, 128), BF16),
            pltpu.VMEM((3, 8, panels), F32),
            pltpu.VMEM((members, 16, panels // 2), BF16),
            pltpu.VMEM((members * clusters + 1, 8, 128), F32),
            pltpu.VMEM((members * regions, clusters, 128), BF16),
            pltpu.VMEM((members * regions * clusters, 128), F32),
            pltpu.VMEM((clusters * 32, 128), F32),
            pltpu.VMEM((clusters, 256, 64), BF16),
            pltpu.VMEM((clusters * 16, 128), F32),
            pltpu.VMEM((128, panels), BF16),
            pltpu.VMEM((clusters * 16, panels), BF16),
            pltpu.VMEM((clusters * 16, panels), BF16),
            pltpu.VMEM((8, panels), F32),
            pltpu.VMEM((2, rows, 4 * panels), BF16),
            pltpu.VMEM((members, rows, 128), BF16),
            pltpu.VMEM((4, rows // 2, 128), F32),
            pltpu.VMEM((4, rows // 2, 128), F32),
            pltpu.VMEM((4, 4, rows // 2, 128), BF16),
            pltpu.VMEM((4, 4, rows // 2, 128), BF16),
            pltpu.VMEM((4, rows, 128), BF16),
            pltpu.VMEM((4, rows, 128), BF16),
            dma((11,)),
            dma((2,)),
            dma((2,)),
            dma((2,)),
            dma((2,)),
            dma((2,)),
            dma((2,)),
            dma((2,)),
            pltpu.SemaphoreType.REGULAR,
        ],
        compiler_params=pltpu.CompilerParams(
            collective_id=0, has_side_effects=True, vmem_limit_bytes=56 * 1024 * 1024
        ),
        name="hull",
    )(
        near_cols,
        near_count,
        far_cols,
        jnp.transpose(velocity, (1, 0, 2)),
        normals,
        areas.reshape(1, panels),
        panel_nodes.T,
        jnp.transpose(basis_v, (0, 2, 1)),
        jnp.transpose(basis_u, (0, 2, 1)),
        near_blocks,
        jnp.transpose(coupling, (0, 2, 3, 1)),
    )
    return jnp.transpose(result, (1, 0, 2))


def solution(mesh):
    both = ("region", "member")
    placed = (
        P(None, None, both),
        P(None, both),
        P(both),
        P(both, None),
        P(both, None, None),
        P(both, None),
        P(both),
        P(both, None, None),
        P(both, None, None),
        P(both, None, None, None),
        P(both, None),
    )
    return jax.shard_map(
        functools.partial(body, mesh.shape["region"], mesh.shape["member"]),
        mesh=mesh,
        in_specs=placed,
        out_specs=P(None, None, both),
        check_vma=False,
    )
```

```python
import functools

import jax
import jax.numpy as jnp
from jax import lax
from jax.experimental import pallas as pl
from jax.experimental.pallas import tpu as pltpu
from jax.sharding import PartitionSpec as P

MESH = pl.DeviceIdType.MESH
F32 = jnp.float32
BF16 = jnp.bfloat16
NT = (((1,), (1,)), ((), ()))


def split(x):
    high = x.astype(BF16)
    return high, (x - high.astype(F32)).astype(BF16)


def dot(a, b):
    return jnp.dot(a, b, preferred_element_type=F32)


def dot_nt(a, b):
    return lax.dot_general(a, b, NT, preferred_element_type=F32)


def kernel(
    regions,
    members,
    near_cols_hbm,
    near_count_hbm,
    far_cols_hbm,
    velocity_hbm,
    normals_hbm,
    areas_hbm,
    nodes_hbm,
    basis_v_hbm,
    basis_u_hbm,
    near_hbm,
    coupling_hbm,
    out,
    near_cols,
    near_count,
    far_cols,
    velocity,
    normals,
    areas,
    nodes,
    basis_v,
    basis_u,
    near,
    coupling,
    hot,
    hot_turned,
    column_of,
    motion,
    motion_cat,
    motion_low,
    moved,
    dens,
    table,
    coeffs,
    coeff_rows,
    picked_rows,
    coup_cat,
    folded,
    basis_v_wide,
    basis_u_high,
    basis_u_low,
    near_pot,
    spread,
    force_out,
    upper_own,
    lower_own,
    upper_in,
    lower_in,
    last_out,
    last_in,
    load_sems,
    motion_sems,
    relay_sems,
    dens_sems,
    coeff_sems,
    side_sems,
    force_sems,
    last_sems,
    ready,
):
    region = lax.axis_index("region")
    me = lax.axis_index("member")
    x, y = me // 4, lax.rem(me, 4)
    plane, core = region // 2, lax.rem(region, 2)
    clusters, block = near.shape[0], near.shape[1]
    panels = nodes.shape[1]
    loads = velocity.shape[1]

    def member_at(step):
        return lax.rem(me + step, members)

    def along_x(turn):
        return lax.rem(x + turn, 4) * 4 + y

    def along_y(turn):
        return x * 4 + lax.rem(y + turn, 4)

    def load(source, target, at):
        return pltpu.make_async_copy(source, target, load_sems.at[at])

    velocity_load = load(velocity_hbm, velocity, 0)
    nodes_load = load(nodes_hbm, nodes, 1)
    near_load = load(near_hbm, near, 2)
    coup_load = load(coupling_hbm, coupling, 3)
    small_loads = [
        load(normals_hbm, normals, 4),
        load(areas_hbm, areas, 5),
        load(basis_v_hbm, basis_v, 6),
        load(basis_u_hbm, basis_u, 7),
        load(near_cols_hbm, near_cols, 8),
        load(near_count_hbm, near_count, 9),
        load(far_cols_hbm, far_cols, 10),
    ]
    velocity_load.start()
    barrier = pltpu.get_barrier_semaphore()
    for turn in range(1, 4):
        for peer in (along_x(turn), along_y(turn)):
            pl.semaphore_signal(barrier, inc=1, device_id=(region, peer), device_id_type=MESH)
    for step in range(1, regions):
        pl.semaphore_signal(
            barrier, inc=1, device_id=(lax.rem(region + step, regions), me), device_id_type=MESH
        )

    nodes_load.start()
    near_load.start()
    coup_load.start()
    for copy in small_loads:
        copy.start()

    def push(source, target, sems, step):
        return push_to(source, target, sems, region, member_at(step))

    def push_all(rows, sems):
        @pl.loop(1, members, unroll=5)
        def _(step):
            push(rows.at[me], rows.at[me], sems, step).start()

    def pushed(rows, sems):
        part = rows.at[pl.ds(0, members - 1)]
        return push(part, part, sems, 1)

    velocity_load.wait()
    own = jnp.concatenate(
        [velocity[c, :, lo * 128 : (lo + 1) * 128] for lo in range(8) for c in range(3)], axis=0
    )
    own_high, own_low = split(own)
    motion[x, y] = own_high
    motion_low[...] = own_low
    pl.semaphore_wait(barrier, 6 + regions - 1)
    half_rows = motion.shape[2] // 2
    upper, lower = pl.ds(0, half_rows), pl.ds(half_rows, half_rows)

    for turn in (2, 1, 3):
        mine = motion.at[x, y, upper]
        push_to(mine, mine, motion_sems, region, along_x(turn)).start()
        mine = motion.at[x, y, lower]
        push_to(mine, mine, motion_sems, region, along_y(turn)).start()

    nodes_load.wait()
    node = nodes[...]
    lanes_low, owner = (node & 127).astype(F32), (node >> 10).astype(F32)
    ahead_x = ((node >> 12) - x) & 3
    ahead_y = (((node >> 10) & 3) - y) & 3
    stand = (((ahead_y - ahead_x + 3) & 3) * 4 + ahead_x).astype(F32)
    column_of[...] = jnp.transpose(jnp.concatenate([lanes_low, stand], axis=0))
    one, zero = jnp.ones((), BF16), jnp.zeros((), BF16)

    @pl.loop(0, 8)
    def _(i):
        base = pl.multiple_of(i * 16, 16)
        rows = (lax.broadcasted_iota(jnp.int32, (16, panels), 0) + base).astype(F32).astype(BF16)
        for k in range(4):
            low = jnp.broadcast_to(lanes_low[k : k + 1], (16, panels)).astype(BF16)
            holder = jnp.broadcast_to(owner[k : k + 1], (16, panels)).astype(BF16)
            found = jnp.where(low == rows, one, zero)
            for m in range(members):
                hot[pl.ds(m * 128 + base, 16), k * panels : (k + 1) * panels] = jnp.where(
                    holder == float(m), found, zero
                )

    firsts = motion.at[0, pl.ds(0, 3)]
    first_pushed = push(firsts, firsts, motion_sems, 1)
    first_pushed.wait_recv()
    for turn in (2, 1, 3):
        line = motion.at[:, y, upper]
        push_to(line, line, relay_sems, region, along_y(turn)).start()
        line = motion.at[x, :, lower]
        push_to(line, line, relay_sems, region, along_x(turn)).start()
    for step in range(1, regions):
        pl.semaphore_signal(
            ready, inc=1, device_id=(lax.rem(region + step, regions), me), device_id_type=MESH
        )
    seconds = motion.at[pl.ds(0, 3)]
    second_pushed = push(seconds, seconds, relay_sems, 1)

    @pl.loop(0, panels // 16)
    def _(i):
        base = pl.multiple_of(i * 16, 16)
        lanes = lax.broadcasted_iota(jnp.int32, (16, 128), 1).astype(F32).astype(BF16)
        for k in range(4):
            low = jnp.broadcast_to(column_of[pl.ds(base, 16), k : k + 1], (16, 128)).astype(BF16)
            holder = jnp.broadcast_to(column_of[pl.ds(base, 16), k + 4 : k + 5], (16, 128)).astype(BF16)
            found = jnp.where(low == lanes, one, zero)
            for m in range(members):
                hot_turned[pl.ds(k * panels + base, 16), m * 128 : (m + 1) * 128] = jnp.where(
                    holder == float(m), found, zero
                )

    for copy in small_loads:
        copy.wait()
    for g in range(clusters // 2):
        pair = jnp.concatenate([basis_v[2 * g], basis_v[2 * g + 1]], axis=1)
        basis_v_wide[:, g * 128 : (g + 1) * 128] = jnp.concatenate([pair] * loads, axis=0)
    basis_u_high[...] = jnp.zeros_like(basis_u_high)
    basis_u_low[...] = jnp.zeros_like(basis_u_low)
    empty = jnp.zeros((16, block), F32)
    for t in range(clusters):
        parts = [basis_u[t], empty] if t % 2 == 0 else [empty, basis_u[t]]
        high, low = split(jnp.concatenate(parts, axis=1))
        where = (slice(t * 16, t * 16 + 16), slice(t // 2 * 128, t // 2 * 128 + 128))
        basis_u_high[where] = high
        basis_u_low[where] = low
    coup_load.wait()

    @pl.loop(0, clusters)
    def _(t):
        high, low = split(coupling[t].reshape(256, 32))
        coup_cat[t] = jnp.concatenate([high, low], axis=1)

    table[table.shape[0] - 1] = jnp.zeros((8, 128), F32)

    second_pushed.wait_recv()
    for m in range(members):
        motion_cat[:, m * 128 : (m + 1) * 128] = motion[m // 4, m % 4]
    own_rows = pl.ds(pl.multiple_of(me * 128, 128), 128)

    for c in range(3):
        moved[c] = jnp.zeros((8, panels), F32)

    @pl.loop(0, 4)
    def _(k):
        columns = pl.ds(pl.multiple_of(k * panels, panels), panels)
        rows = dot(motion_cat[...], hot[:, columns]) + dot(motion_low[...], hot[own_rows, columns])
        lo = (nodes[pl.ds(k, 1), :] >> 7) & 7
        for c in range(3):
            total = moved[c]
            for q in range(8):
                at = (q * 3 + c) * 8
                total = total + jnp.where(jnp.broadcast_to(lo == q, (8, panels)), rows[at : at + 8], 0.0)
            moved[c] = total

    normal_vel = 0.25 * (
        moved[0] * normals[0:1, :] + moved[1] * normals[1:2, :] + moved[2] * normals[2:3, :]
    )
    density = normal_vel.astype(BF16).astype(F32)
    half = panels // 2
    dens[me] = jnp.concatenate([density[:, :half], density[:, half:]], axis=0).astype(BF16)
    lane_cluster = lax.broadcasted_iota(jnp.int32, (8, panels), 1) // block
    diagonal = jnp.concatenate(
        [jnp.where(lane_cluster == t, density, 0.0) for t in range(clusters)], axis=0
    ).astype(BF16)
    wide = dot_nt(diagonal, basis_v_wide[...])
    row_load = lax.broadcasted_iota(jnp.int32, (128, 128), 0) & 7
    lane_load = lax.broadcasted_iota(jnp.int32, (128, 128), 1) >> 4
    wide = jnp.where(row_load == lane_load, wide, 0.0)
    device = (core * (regions // 2) + plane) * members + me
    coeffs[device] = jnp.sum(wide.reshape(clusters, 8, 128), axis=1).astype(BF16)
    pl.semaphore_wait(ready, regions - 1)
    chips = regions // 2 * members

    @pl.loop(1, chips, unroll=7)
    def _(turn):
        step = chips - turn
        there = lax.rem(plane + step // members, regions // 2) * 2 + core
        push_to(coeffs.at[device], coeffs.at[device], coeff_sems, there, member_at(lax.rem(step, members))).start()

    push_all(dens, dens_sems)

    coeff_part = coeffs.at[pl.ds(0, chips - 1)]
    coeff_pushed = push(coeff_part, coeff_part, coeff_sems, 1)
    coeff_pushed.wait_recv()
    side = coeffs.at[pl.ds(pl.multiple_of(core * chips, chips), chips)]
    side_pushed = push_to(side, side, side_sems, region + 1 - 2 * core, me)
    side_pushed.start()
    near_load.wait()
    pushed(dens, dens_sems).wait_recv()
    left = lax.broadcasted_iota(jnp.int32, (8, 128), 1) < block

    @pl.loop(0, members, unroll=16)
    def _(m):
        rows = dens[m].astype(F32)
        for h in range(2):
            for g in range(half // 128):
                both = rows[h * 8 : h * 8 + 8, g * 128 : (g + 1) * 128]
                turned = pltpu.roll(both, block, axis=1)
                at = m * clusters + h * (clusters // 2) + g * 2
                table[at] = jnp.where(left, both, turned)
                table[at + 1] = jnp.where(left, turned, both)

    slots = near_cols.shape[1]
    unused = table.shape[0] - 1

    def near_pair(g):
        picked = []
        for h in range(2):
            t = 2 * g + h
            count = near_count[t]
            parts = []
            for j in range(0, slots, 2):
                first = jnp.where(j < count, near_cols[t, j], unused)
                second = jnp.where(j + 1 < count, near_cols[t, j + 1], unused)
                parts.append(jnp.where(left, table[first], table[second]))
            picked.append(jnp.concatenate(parts, axis=1))
        both = jnp.concatenate(picked, axis=0).astype(BF16)
        blocks = near[pl.ds(2 * g, 2)].reshape(2 * block, slots * block)
        result = dot_nt(both, blocks)
        near_pot[:, pl.ds(pl.multiple_of(g * 128, 128), 128)] = jnp.where(left, result[:8], result[8:])

    @pl.loop(0, clusters // 2, unroll=8)
    def _(g):
        near_pair(g)

    side_pushed.wait_recv()

    @pl.loop(0, members, unroll=2)
    def _(i):
        for r in range(regions):
            at = pl.multiple_of((r * members + i) * clusters, clusters)
            d = (r % 2 * (regions // 2) + r // 2) * members + i
            coeff_rows[pl.ds(at, clusters), :] = coeffs[d].astype(F32)

    own_q = lax.broadcasted_iota(jnp.int32, (256, 128), 0) & 15
    lane_q = lax.broadcasted_iota(jnp.int32, (256, 128), 1) & 15
    same_q = own_q == lane_q

    @pl.loop(0, clusters, unroll=4)
    def _(t):
        for a in range(32):
            picked_rows[pl.ds(t * 32 + a, 1), :] = coeff_rows[pl.ds(far_cols[t, a], 1), :]

    for t in range(clusters):
        rows = picked_rows[t * 32 : t * 32 + 32].astype(BF16)
        product = dot(coup_cat[t], jnp.concatenate([rows, rows], axis=0))
        product = jnp.where(same_q, product, 0.0)
        folded[t * 16 : t * 16 + 16] = jnp.sum(product.reshape(16, 16, 128), axis=1)

    fold = jnp.where(
        lax.broadcasted_iota(jnp.int32, (8, 128), 0)
        == lax.broadcasted_iota(jnp.int32, (8, 128), 1) >> 4,
        1.0,
        0.0,
    )
    fold = jnp.concatenate([fold, fold], axis=0).astype(BF16)
    folded_high, folded_low = split(folded[...])
    far_coef = (dot_nt(fold, folded_high) + dot_nt(fold, folded_low))[:8]
    far_high, far_low = split(far_coef)
    far_both = jnp.concatenate([far_high.astype(F32), far_low.astype(F32)], axis=0).astype(BF16)
    with_high = dot(far_both, basis_u_high[...])
    with_low = dot(far_both, basis_u_low[...])
    potential = near_pot[...] + (with_high[:8] + with_high[8:] + with_low[:8])

    scaled = -0.25 * areas[...]
    for c in range(3):
        moved[c] = potential * (scaled * normals[c : c + 1, :])

    def build_spread(at):
        @pl.loop(0, panels // 256)
        def _(i):
            base = pl.multiple_of(i * 256, 256)
            load = [moved[c, :, pl.ds(base, 256)] for c in range(3)]
            for k in range(4):
                lo = (nodes[k : k + 1, pl.ds(base, 256)] >> 7) & 7
                rows = []
                for q in range(8):
                    hit = jnp.broadcast_to(lo == q, (8, 256))
                    rows += [jnp.where(hit, load[c], 0.0) for c in range(3)]
                columns = pl.ds(k * panels + base, 256)
                spread[at, :, columns] = jnp.concatenate(rows, axis=0).astype(BF16)

    build_spread(0)

    partial = force_out.at[pl.ds(0, 12)]
    partial_pushed = push(partial, partial, force_sems, 1)

    def upper_sum(to_y):
        total = upper_own[to_y]
        for turn in range(1, 4):
            total = total + upper_in[lax.rem(x + turn, 4), to_y].astype(F32)
        return total

    def lower_sum(to_x):
        total = lower_own[to_x]
        for turn in range(1, 4):
            total = total + lower_in[lax.rem(y + turn, 4), to_x].astype(F32)
        return total

    def second_hop():
        partial_pushed.wait_recv()
        for turn in (2, 1, 3):
            last_out[turn, upper] = upper_sum(lax.rem(y + turn, 4)).astype(BF16)
            piece = (last_out.at[turn, upper], last_in.at[turn, upper])
            push_to(*piece, last_sems, region, along_y(turn)).start()
            last_out[turn, lower] = lower_sum(lax.rem(x + turn, 4)).astype(BF16)
            piece = (last_out.at[turn, lower], last_in.at[turn, lower])
            push_to(*piece, last_sems, region, along_x(turn)).start()

    @pl.loop(0, 5)
    def _(i):
        @pl.when(i == 4)
        def _():
            second_hop()
            for c in range(3):
                moved[c] = moved[c] - moved[c].astype(BF16).astype(F32)
            build_spread(1)

        columns = pl.ds(pl.multiple_of((i - i // 4) * 512, 512), 512)
        sums = dot(spread[i // 4], hot_turned[:, columns])

        @pl.when(i < 4)
        def _():
            for h in range(4):
                ahead = lax.rem(h + i + 1, 4)
                to_x, to_y = lax.rem(x + h, 4), lax.rem(y + ahead, 4)
                at = i * 4 + h
                sums_of = sums[:, h * 128 : (h + 1) * 128]
                force_out[at] = sums_of.astype(BF16)
                if h == 0:
                    upper_own[to_y] = sums_of[:half_rows]
                else:
                    push_to(
                        force_out.at[at, upper], upper_in.at[x, to_y], force_sems, region, to_x * 4 + y
                    ).start()

                @pl.when(ahead == 0)
                def _():
                    lower_own[to_x] = sums_of[half_rows:]

                @pl.when(ahead != 0)
                def _():
                    push_to(
                        force_out.at[at, lower], lower_in.at[y, to_x], force_sems, region, x * 4 + to_y
                    ).start()

        @pl.when(i == 4)
        def _():
            upper_own[y] += sums[:half_rows, :128]
            lower_own[x] += sums[half_rows:, :128]

    total = jnp.concatenate([upper_sum(y), lower_sum(x)], axis=0)
    last = last_out.at[pl.ds(1, 3)]
    last_pushed = push(last, last, last_sems, 1)
    last_pushed.wait_recv()
    for turn in range(1, 4):
        total = total + last_in[turn].astype(F32)
    for lo in range(8):
        for c in range(3):
            at = (lo * 3 + c) * 8
            out[c, :, lo * 128 : (lo + 1) * 128] = total[at : at + 8]

    first_pushed.wait_send()
    second_pushed.wait_send()
    pushed(dens, dens_sems).wait_send()
    coeff_pushed.wait_send()
    side_pushed.wait_send()
    partial_pushed.wait_send()
    last_pushed.wait_send()


def push_to(source, target, sems, region, member):
    return pltpu.make_async_remote_copy(
        src_ref=source,
        dst_ref=target,
        send_sem=sems.at[0],
        recv_sem=sems.at[1],
        device_id=(region, member),
        device_id_type=MESH,
    )


def body(
    regions,
    members,
    velocity,
    normals,
    areas,
    panel_nodes,
    near_blocks,
    near_cols,
    near_count,
    basis_v,
    basis_u,
    coupling,
    far_cols,
):
    nodes = velocity.shape[2]
    panels = normals.shape[1]
    clusters, block = near_blocks.shape[0], near_blocks.shape[1]
    rows = 24 * nodes // 128
    lanes = members * 128
    vmem = pl.BlockSpec(memory_space=pltpu.VMEM)
    hbm = pl.BlockSpec(memory_space=pl.ANY)
    dma = pltpu.SemaphoreType.DMA
    result = pl.pallas_call(
        functools.partial(kernel, regions, members),
        out_shape=pltpu.VMEM((3, 8, nodes), F32),
        in_specs=[hbm] * 11,
        out_specs=vmem,
        scratch_shapes=[
            pltpu.SMEM(near_cols.shape, jnp.int32),
            pltpu.SMEM(near_count.shape, jnp.int32),
            pltpu.SMEM(far_cols.shape, jnp.int32),
            pltpu.VMEM((3, 8, nodes), F32),
            pltpu.VMEM(normals.shape, F32),
            pltpu.VMEM((1, panels), F32),
            pltpu.VMEM((4, panels), jnp.int32),
            pltpu.VMEM((clusters, 16, block), BF16),
            pltpu.VMEM((clusters, 16, block), F32),
            pltpu.VMEM(near_blocks.shape, BF16),
            pltpu.VMEM((clusters, 16, 16, 32), F32),
            pltpu.VMEM((lanes, 4 * panels), BF16),
            pltpu.VMEM((4 * panels, lanes), BF16),
            pltpu.VMEM((panels, 8), F32),
            pltpu.VMEM((4, 4, rows, 128), BF16),
            pltpu.VMEM((rows, lanes), BF16),
            pltpu.VMEM((rows, 128), BF16),
            pltpu.VMEM((3, 8, panels), F32),
            pltpu.VMEM((members, 16, panels // 2), BF16),
            pltpu.VMEM((members * clusters + 1, 8, 128), F32),
            pltpu.VMEM((members * regions, clusters, 128), BF16),
            pltpu.VMEM((members * regions * clusters, 128), F32),
            pltpu.VMEM((clusters * 32, 128), F32),
            pltpu.VMEM((clusters, 256, 64), BF16),
            pltpu.VMEM((clusters * 16, 128), F32),
            pltpu.VMEM((128, panels), BF16),
            pltpu.VMEM((clusters * 16, panels), BF16),
            pltpu.VMEM((clusters * 16, panels), BF16),
            pltpu.VMEM((8, panels), F32),
            pltpu.VMEM((2, rows, 4 * panels), BF16),
            pltpu.VMEM((members, rows, 128), BF16),
            pltpu.VMEM((4, rows // 2, 128), F32),
            pltpu.VMEM((4, rows // 2, 128), F32),
            pltpu.VMEM((4, 4, rows // 2, 128), BF16),
            pltpu.VMEM((4, 4, rows // 2, 128), BF16),
            pltpu.VMEM((4, rows, 128), BF16),
            pltpu.VMEM((4, rows, 128), BF16),
            dma((11,)),
            dma((2,)),
            dma((2,)),
            dma((2,)),
            dma((2,)),
            dma((2,)),
            dma((2,)),
            dma((2,)),
            pltpu.SemaphoreType.REGULAR,
        ],
        compiler_params=pltpu.CompilerParams(
            collective_id=0, has_side_effects=True, vmem_limit_bytes=56 * 1024 * 1024
        ),
        name="hull",
    )(
        near_cols,
        near_count,
        far_cols,
        jnp.transpose(velocity, (1, 0, 2)),
        normals,
        areas.reshape(1, panels),
        panel_nodes.T,
        jnp.transpose(basis_v, (0, 2, 1)),
        jnp.transpose(basis_u, (0, 2, 1)),
        near_blocks,
        jnp.transpose(coupling, (0, 2, 3, 1)),
    )
    return jnp.transpose(result, (1, 0, 2))


def solution(mesh):
    both = ("region", "member")
    placed = (
        P(None, None, both),
        P(None, both),
        P(both),
        P(both, None),
        P(both, None, None),
        P(both, None),
        P(both),
        P(both, None, None),
        P(both, None, None),
        P(both, None, None, None),
        P(both, None),
    )
    return jax.shard_map(
        functools.partial(body, mesh.shape["region"], mesh.shape["member"]),
        mesh=mesh,
        in_specs=placed,
        out_specs=P(None, None, both),
        check_vma=False,
    )
```
